256 devices in a mesh: seq: 64 (over z, y, core), tp: 4 (over x).
Axes of the slice: x: 4, y: 4, z: 8, core: 2. Of those that a mesh axis runs over, the one named last changes fastest.
Arguments:
- text_query_matrix: bfloat16 [16384, 8192], P('seq', 'tp'), may hold values from -12 to 12
- vision: bfloat16 [16384, 8192], P(('seq', 'tp')), may hold values from -12 to 12
- key_matrix: bfloat16 [8192, 1024], P(None, 'tp'), may hold values from -0.0625 to 0.0625
- value_matrix: bfloat16 [8192, 1024], P(None, 'tp'), may hold values from -0.0625 to 0.0625
- query_norm_gain: float32 [128], replicated, may hold values from 0.5 to 1.5
- key_gain: float32 [128], replicated, may hold values from 0.5 to 1.5
- block_mask: int32 [256, 64], P('seq'), may hold values from 0 to 1, as said below
Outputs:
- attended: bfloat16 [16384, 8192], P('seq', 'tp')
The draws below stay inside these ranges and needn't reach their ends.
Inputs may be any that keep to these rules, and one draw needn't show every extreme that they name: block_mask[b, i] is 1 on exactly one run of consecutive blocks b; the run starts in the blocks of text shard i (blocks i * 4 to (i + 1) * 4 - 1) and ends at or before the last block of text shard i + 3; in every draw some image's run ends exactly at that last block.
All inputs are finite; a program needn't handle non-finite values.
Results may differ from the reference program's by a relative error of at most 0.0076.
Values may be sent and summed in bfloat16 or wider, within the bound.
No kernel may reach another device: no remote copies, remote signals or barrier semaphores. Data moves between devices by JAX's collectives and lax.ppermute only.
A program may use at most 128 MiB of HBM per device.

```python
import jax
import jax.numpy as jnp
from jax import lax

QUERY_HEADS = 64
KEY_VALUE_HEADS = 8
HEAD_SIZE = 128
VISION_WIDTH = 8192
TXT_DEV = 256
IMAGE_TOKENS = 256
REACH = 4
BLOCK = 64
TEXT_TOKENS = 16384
IMAGE_COUNT = 64
NBLK = 256
N_SEQ = 64


def rough_rows(key, shape):
    first = jax.random.fold_in(key, 0)
    base = jnp.clip(jax.random.normal(first, shape, jnp.float32), -4.0, 4.0)
    return base


def draw_text_query_matrix(key, part):
    return rough_rows(jax.random.fold_in(key, 11), (TEXT_TOKENS, QUERY_HEADS * HEAD_SIZE)).astype(jnp.bfloat16)


def draw_vision(key, part):
    return rough_rows(jax.random.fold_in(key, 23), (IMAGE_COUNT * IMAGE_TOKENS, VISION_WIDTH)).astype(jnp.bfloat16)


def draw_block_mask(key, part):
    per_shard_blocks = TXT_DEV // BLOCK
    first, second, third = jax.random.split(jax.random.fold_in(key, 37), 3)
    image_index = jnp.arange(IMAGE_COUNT, dtype=jnp.int32)
    offset = jax.random.randint(first, (IMAGE_COUNT,), 0, per_shard_blocks, jnp.int32)
    start = image_index * per_shard_blocks + offset
    room = REACH * per_shard_blocks - offset
    length = 1 + jax.random.randint(second, (IMAGE_COUNT,), 0, 1 << 20, jnp.int32) % room
    forced = jax.random.randint(third, (), 0, IMAGE_COUNT - REACH + 1, jnp.int32)
    length = jnp.where(image_index == forced, room, length)
    blocks = jnp.arange(NBLK, dtype=jnp.int32)[:, None]
    inside = (blocks >= start[None, :]) & (blocks < (start + length)[None, :])
    return inside.astype(jnp.int32)


def levels(rng, shape, cuts, least, largest):
    level, own = 1.0, jax.random.fold_in(rng, 6)
    for axis_at, shards_of in cuts:
        heights = jnp.exp(jax.random.uniform(jax.random.fold_in(own, axis_at), (shards_of,), jnp.float32, least / len(cuts), largest / len(cuts)))
        level = level * jnp.repeat(heights, shape[axis_at] // shards_of).reshape([-1 if axis == axis_at else 1 for axis in range(len(shape))])
    return level


def bell_draw(rng, shape, spread, bound, cuts=(), held_as=jnp.bfloat16):
    result = jax.random.normal(rng, shape, jnp.float32) * spread
    if len(cuts) > 0:
        result = levels(rng, shape, cuts, -0.22, 0.18) * result
    return jnp.clip(result, min=-bound, max=bound).astype(held_as)


def setup_inputs(seed: int = 0) -> dict:
    splits = jax.random.split(jax.random.key(seed), 8)
    return {
        "text_query_matrix": draw_text_query_matrix(jax.random.fold_in(splits[7], 71), 0),
        "vision": draw_vision(jax.random.fold_in(splits[7], 71), 0),
        "key_matrix": bell_draw(splits[2], (VISION_WIDTH, KEY_VALUE_HEADS * HEAD_SIZE), VISION_WIDTH ** -0.5, 0.0625, ((1, 4),)),
        "value_matrix": bell_draw(splits[3], (VISION_WIDTH, KEY_VALUE_HEADS * HEAD_SIZE), VISION_WIDTH ** -0.5, 0.0625, ((1, 4),)),
        "query_norm_gain": jnp.clip(1.0 + 0.1 * jax.random.normal(splits[4], (HEAD_SIZE,), jnp.float32), 0.5, 1.5),
        "key_gain": jnp.clip(1.0 + 0.1 * jax.random.normal(splits[5], (HEAD_SIZE,), jnp.float32), 0.5, 1.5),
        "block_mask": draw_block_mask(jax.random.fold_in(splits[7], 71), 0),
    }


def heads_normalized(tensor, scale_gain):
    return tensor * lax.rsqrt(lax.optimization_barrier(jnp.mean(tensor * tensor, axis=-1, keepdims=True)) + 1e-05) * scale_gain

def reference(text_query_matrix, vision, key_matrix, value_matrix, query_norm_gain, key_gain, block_mask):
    query_group_width = QUERY_HEADS // KEY_VALUE_HEADS
    per_shard_blocks = TXT_DEV // BLOCK
    score_scale = HEAD_SIZE ** (-0.5)
    key_projected = jnp.dot(vision, key_matrix, preferred_element_type=jnp.float32).reshape(IMAGE_COUNT * IMAGE_TOKENS, KEY_VALUE_HEADS, HEAD_SIZE)
    key_matrix_rows = heads_normalized(key_projected, key_gain).astype(jnp.bfloat16)
    value_matrix_rows = jnp.dot(vision, value_matrix, preferred_element_type=jnp.float32).astype(jnp.bfloat16).reshape(IMAGE_COUNT * IMAGE_TOKENS, KEY_VALUE_HEADS, HEAD_SIZE)
    normalized_query = heads_normalized(text_query_matrix.astype(jnp.float32).reshape(TEXT_TOKENS, KEY_VALUE_HEADS, query_group_width, HEAD_SIZE), query_norm_gain).astype(jnp.bfloat16)
    leading_part = (REACH - 1) * IMAGE_TOKENS
    key_extended = jnp.concatenate([jnp.zeros((leading_part, KEY_VALUE_HEADS, HEAD_SIZE), jnp.bfloat16), key_matrix_rows], axis=0)
    value_extended = jnp.concatenate([jnp.zeros((leading_part, KEY_VALUE_HEADS, HEAD_SIZE), jnp.bfloat16), value_matrix_rows], axis=0)
    mask_padded = jnp.concatenate([jnp.zeros((NBLK, REACH - 1), jnp.int32), block_mask.astype(jnp.int32)], axis=1)

    def per_shard(index):
        query_block = lax.dynamic_slice_in_dim(normalized_query, (index * TXT_DEV).astype(jnp.int32), TXT_DEV, 0)
        key_block = lax.dynamic_slice_in_dim(key_extended, (index * IMAGE_TOKENS).astype(jnp.int32), REACH * IMAGE_TOKENS, 0)
        value_block = lax.dynamic_slice_in_dim(value_extended, (index * IMAGE_TOKENS).astype(jnp.int32), REACH * IMAGE_TOKENS, 0)
        mask_block = lax.dynamic_slice(mask_padded, ((index * per_shard_blocks).astype(jnp.int32), index.astype(jnp.int32)), (per_shard_blocks, REACH))
        mask_tokens = jnp.repeat(jnp.repeat(mask_block.astype(jnp.float32), BLOCK, axis=0), IMAGE_TOKENS, axis=1)
        scores = jnp.einsum('tgid,kgd->gitk', query_block.astype(jnp.float32), key_block.astype(jnp.float32)) * score_scale
        weights = jnp.exp(scores) * mask_tokens[None, None]
        totals = lax.optimization_barrier(jnp.sum(weights, axis=-1))
        rounded = weights.astype(jnp.bfloat16).astype(jnp.float32)
        summed = jnp.einsum('gitk,kgd->tgid', rounded, value_block.astype(jnp.float32))
        totals_t = jnp.transpose(totals, (2, 0, 1))[..., None]
        has_image = totals_t > 0
        averaged = summed / jnp.where(has_image, totals_t, jnp.ones_like(totals_t))
        result_rows = jnp.where(has_image, averaged, jnp.zeros_like(averaged))
        return result_rows.astype(jnp.bfloat16).reshape(TXT_DEV, QUERY_HEADS * HEAD_SIZE)
    every_shard = lax.map(per_shard, jnp.arange(N_SEQ, dtype=jnp.int32))
    return every_shard.reshape(TEXT_TOKENS, QUERY_HEADS * HEAD_SIZE)
```

```python
import functools
import math

import jax
import jax.numpy as jnp
from jax import lax
from jax.experimental import pallas as pl
from jax.experimental.pallas import tpu as pltpu
from jax.sharding import PartitionSpec as P

HEAD_SIZE = 128
REACH = 4
BLOCK = 64
EPS = 1e-05
SCORE_SCALE = HEAD_SIZE ** (-0.5) * math.log2(math.e)
VMEM_LIMIT = 48 * 1024 * 1024


def shifted(value, axis, by):
    length = lax.axis_size(axis)
    pairs = [(i, i + by) for i in range(length) if 0 <= i + by < length]
    return lax.ppermute(value, axis, pairs)


def turned(value, axis, by):
    length = lax.axis_size(axis)
    return lax.ppermute(value, axis, [(i, (i + by) % length) for i in range(length)])


def project_kernel(count, *refs):
    row_refs = refs[:count]
    key_ref, value_ref, gain_ref, out_ref, total = refs[count:]
    step = pl.program_id(0)
    width = key_ref.shape[1]
    rows = [ref[...] for ref in row_refs]
    rows = rows[0] if count == 1 else jnp.concatenate(rows, axis=0)

    @pl.when(step == 0)
    def _():
        total[...] = jnp.zeros_like(total)

    total[:, :width] += jnp.dot(rows, key_ref[...], preferred_element_type=jnp.float32)
    total[:, width:] += jnp.dot(rows, value_ref[...], preferred_element_type=jnp.float32)

    @pl.when(step == pl.num_programs(0) - 1)
    def _():
        for head in range(width // HEAD_SIZE):
            at = slice(head * HEAD_SIZE, (head + 1) * HEAD_SIZE)
            keys = total[:, at]
            mean = jnp.mean(keys * keys, axis=-1, keepdims=True)
            out_ref[:, at] = (keys * lax.rsqrt(mean + EPS) * gain_ref[...]).astype(out_ref.dtype)
        out_ref[:, width:] = total[:, width:].astype(out_ref.dtype)


def project(row_parts, key_matrix, value_matrix, key_gain, name):
    depth, width = key_matrix.shape
    part = depth // 8
    rows = sum(each.shape[0] for each in row_parts)
    return pl.pallas_call(
        functools.partial(project_kernel, len(row_parts)),
        out_shape=jax.ShapeDtypeStruct((rows, 2 * width), jnp.bfloat16),
        grid=(depth // part,),
        in_specs=[pl.BlockSpec((each.shape[0], part), lambda i: (0, i)) for each in row_parts]
        + [pl.BlockSpec((part, width), lambda i: (i, 0))] * 2
        + [pl.BlockSpec((1, HEAD_SIZE), lambda i: (0, 0))],
        out_specs=pl.BlockSpec((rows, 2 * width), lambda i: (0, 0)),
        scratch_shapes=[pltpu.VMEM((rows, 2 * width), jnp.float32)],
        compiler_params=pltpu.CompilerParams(vmem_limit_bytes=VMEM_LIMIT),
        name=name,
    )(*row_parts, key_matrix, value_matrix, key_gain)


def attend_kernel(first, last, group, *refs):
    refs = list(refs)
    query_ref = refs.pop(0)
    key_refs = [refs.pop(0) for _ in range(REACH)]
    value_refs = [refs.pop(0) for _ in range(REACH)]
    open_ref = refs.pop(0)
    if first:
        gain_ref, normed_ref = refs.pop(0), refs.pop(0)
    else:
        sums_in, totals_in = refs.pop(0), refs.pop(0)
    rows = query_ref.shape[0]
    count = key_refs[0].shape[0]
    keys = jnp.concatenate([ref[...] for ref in key_refs], axis=0)
    values = jnp.concatenate([ref[...] for ref in value_refs], axis=0)
    values = jnp.concatenate([values, jnp.ones_like(values)], axis=1)
    image = lax.broadcasted_iota(jnp.int32, (rows, REACH * count), 1) // count
    is_open = jnp.zeros((rows, REACH * count), jnp.float32)
    for at in range(REACH):
        is_open = jnp.where(image == at, open_ref[:, at : at + 1], is_open)
    lane = lax.broadcasted_iota(jnp.int32, (rows, HEAD_SIZE), 1)
    totals = jnp.zeros((rows, HEAD_SIZE), jnp.float32)
    for head in range(group):
        at = slice(head * HEAD_SIZE, (head + 1) * HEAD_SIZE)
        if first:
            raw = query_ref[:, at].astype(jnp.float32)
            mean = jnp.mean(raw * raw, axis=-1, keepdims=True)
            query = (raw * lax.rsqrt(mean + EPS) * gain_ref[...]).astype(jnp.bfloat16)
            normed_ref[:, at] = query
        else:
            query = query_ref[:, at]
        scores = lax.dot_general(
            query, keys, (((1,), (1,)), ((), ())), preferred_element_type=jnp.float32
        )
        weights = (jnp.exp2(scores) * is_open).astype(jnp.bfloat16)
        both = jnp.dot(weights, values, preferred_element_type=jnp.float32)
        sums, total = both[:, :HEAD_SIZE], both[:, HEAD_SIZE:]
        if not first:
            sums = sums + sums_in[:, at]
            total = total + totals_in[:, head : head + 1]
        if last:
            has_image = total > 0
            safe = jnp.where(has_image, total, jnp.ones_like(total))
            result = jnp.where(has_image, sums / safe, jnp.zeros_like(sums))
            refs[0][:, at] = result.astype(jnp.bfloat16)
        else:
            refs[0][:, at] = sums
            totals = jnp.where(lane == head, total, totals)
    if not last:
        refs[1][...] = totals


def attend(query, blocks, is_open, gain, carried, last, name):
    first = carried is None
    rows, width = query.shape
    count = blocks[0].shape[0]
    kv_heads = blocks[0].shape[1] // (2 * HEAD_SIZE)
    wide = width // kv_heads
    query_spec = pl.BlockSpec((rows, wide), lambda i: (0, i))
    totals_spec = pl.BlockSpec((rows, HEAD_SIZE), lambda i: (0, i))
    in_specs = [query_spec]
    in_specs += [pl.BlockSpec((count, HEAD_SIZE), lambda i: (0, i))] * REACH
    in_specs += [pl.BlockSpec((count, HEAD_SIZE), lambda i: (0, kv_heads + i))] * REACH
    in_specs += [pl.BlockSpec((rows, REACH), lambda i: (0, 0))]
    operands = [query, *blocks, *blocks, is_open]
    if first:
        in_specs += [pl.BlockSpec((1, HEAD_SIZE), lambda i: (0, 0))]
        operands += [gain]
    else:
        in_specs += [query_spec, totals_spec]
        operands += list(carried)
    if last:
        out_shape = [jax.ShapeDtypeStruct((rows, width), jnp.bfloat16)]
        out_specs = [query_spec]
    else:
        out_shape = [
            jax.ShapeDtypeStruct((rows, width), jnp.float32),
            jax.ShapeDtypeStruct((rows, kv_heads * HEAD_SIZE), jnp.float32),
        ]
        out_specs = [query_spec, totals_spec]
    if first:
        out_shape.insert(0, jax.ShapeDtypeStruct((rows, width), jnp.bfloat16))
        out_specs.insert(0, query_spec)
    return pl.pallas_call(
        functools.partial(attend_kernel, first, last, wide // HEAD_SIZE),
        out_shape=out_shape,
        grid=(kv_heads,),
        in_specs=in_specs,
        out_specs=out_specs,
        compiler_params=pltpu.CompilerParams(vmem_limit_bytes=VMEM_LIMIT),
        name=name,
    )(*operands)


def body(
    text_query_matrix, vision, key_matrix, value_matrix, query_norm_gain, key_gain, block_mask
):
    position = lax.axis_index("seq")
    rows = text_query_matrix.shape[0]
    images = lax.broadcasted_iota(jnp.int32, (1, block_mask.shape[1], REACH), 1)
    wanted = position - lax.broadcasted_iota(jnp.int32, (1, block_mask.shape[1], REACH), 2)
    is_open = jnp.sum(jnp.where(images == wanted, block_mask[:, :, None], 0), axis=1)
    is_open = jnp.repeat(is_open.astype(jnp.float32), BLOCK, axis=0)
    query_gain = (query_norm_gain * SCORE_SCALE).reshape(1, HEAD_SIZE)
    key_gain = key_gain.reshape(1, HEAD_SIZE)

    half = vision.shape[0] // 2
    upper, lower = vision[:half], vision[half:]
    upper_left = turned(upper, "tp", 1)
    lower_right = turned(lower, "tp", -1)
    lower_left = turned(lower, "tp", 1)
    upper_right = turned(upper, "tp", -1)
    upper_across = turned(upper_left, "tp", 1)
    lower_across = turned(lower_right, "tp", -1)

    def reached(row_parts, name):
        own = project(row_parts, key_matrix, value_matrix, key_gain, "project_" + name)
        return [own] + [shifted(own, "seq", by) for by in range(1, REACH)]

    own = reached([vision], "own")
    normed, *carried = attend(
        text_query_matrix, own, is_open, query_gain, None, False, "attend_own"
    )
    sides = reached([upper_left, lower_left, upper_right, lower_right], "sides")
    carried = attend(normed, sides, is_open, None, carried, False, "attend_sides")
    across = reached([upper_across, lower_across], "across")
    (result,) = attend(normed, across, is_open, None, carried, True, "attend_across")
    return result


def solution(mesh):
    placed = (
        P("seq", "tp"),
        P(("seq", "tp"), None),
        P(None, "tp"),
        P(None, "tp"),
        P(),
        P(),
        P("seq", None),
    )
    return jax.shard_map(
        body, mesh=mesh, in_specs=placed, out_specs=P("seq", "tp"), check_vma=False
    )
```

```python
import functools
import math

import jax
import jax.numpy as jnp
from jax import lax
from jax.experimental import pallas as pl
from jax.experimental.pallas import tpu as pltpu
from jax.sharding import PartitionSpec as P

HEAD_SIZE = 128
REACH = 4
BLOCK = 64
EPS = 1e-05
SCORE_SCALE = HEAD_SIZE ** (-0.5) * math.log2(math.e)
PROJECT_VMEM = 8 * 1024 * 1024
ATTEND_VMEM = 20 * 1024 * 1024
WHOLE = pl.BlockSpec(memory_space=pltpu.VMEM)


def shifted(value, axis, by):
    length = lax.axis_size(axis)
    pairs = [(i, i + by) for i in range(length) if 0 <= i + by < length]
    return lax.ppermute(value, axis, pairs)


def turned(value, axis, by):
    length = lax.axis_size(axis)
    return lax.ppermute(value, axis, [(i, (i + by) % length) for i in range(length)])


def project_rows(row_refs, key_ref, value_ref, gain_ref, out_ref):
    width = key_ref.shape[1]
    rows = [ref[...] for ref in row_refs]
    rows = rows[0] if len(rows) == 1 else jnp.concatenate(rows, axis=0)
    keys = jnp.dot(rows, key_ref[...], preferred_element_type=jnp.float32)
    values = jnp.dot(rows, value_ref[...], preferred_element_type=jnp.float32)
    for head in range(width // HEAD_SIZE):
        at = slice(head * HEAD_SIZE, (head + 1) * HEAD_SIZE)
        own = keys[:, at]
        mean = jnp.mean(own * own, axis=-1, keepdims=True)
        out_ref[:, at] = (own * lax.rsqrt(mean + EPS) * gain_ref[...]).astype(out_ref.dtype)
    out_ref[:, width:] = values.astype(out_ref.dtype)


def project_cost(rows, key_matrix):
    size = math.prod(key_matrix.shape)
    return pl.CostEstimate(flops=4 * rows * size, transcendentals=0, bytes_accessed=4 * size)


def project_kernel(*refs):
    *row_refs, key_ref, value_ref, gain_ref, out_ref = refs
    project_rows(row_refs, key_ref, value_ref, gain_ref, out_ref)


def project(row_parts, key_matrix, value_matrix, key_gain, name):
    width = key_matrix.shape[1]
    rows = sum(each.shape[0] for each in row_parts)
    return pl.pallas_call(
        project_kernel,
        out_shape=jax.ShapeDtypeStruct((rows, 2 * width), jnp.bfloat16),
        in_specs=[WHOLE] * (len(row_parts) + 3),
        out_specs=WHOLE,
        cost_estimate=project_cost(rows, key_matrix),
        compiler_params=pltpu.CompilerParams(vmem_limit_bytes=PROJECT_VMEM),
        name=name,
    )(*row_parts, key_matrix, value_matrix, key_gain)


def attend_kernel(first, last, kv_heads, *refs):
    refs = list(refs)
    query_ref = refs.pop(0)
    block_refs = [refs.pop(0) for _ in range(REACH)]
    open_ref = refs.pop(0)
    if first:
        gain_ref, normed_ref = refs.pop(0), refs.pop(0)
    else:
        sums_in, totals_in = refs.pop(0), refs.pop(0)
    rows = query_ref.shape[0]
    count = block_refs[0].shape[0]
    group = query_ref.shape[1] // HEAD_SIZE // kv_heads
    image = lax.broadcasted_iota(jnp.int32, (rows, REACH * count), 1) // count
    is_open = jnp.zeros((rows, REACH * count), jnp.float32)
    for at in range(REACH):
        is_open = jnp.where(image == at, open_ref[:, at : at + 1], is_open)
    is_open = jnp.concatenate([is_open] * group, axis=0)
    lane = lax.broadcasted_iota(jnp.int32, (rows, HEAD_SIZE), 1)
    totals = jnp.zeros((rows, HEAD_SIZE), jnp.float32)

    def columns(head):
        return slice(head * HEAD_SIZE, (head + 1) * HEAD_SIZE)

    for kv_head in range(kv_heads):
        heads = range(kv_head * group, (kv_head + 1) * group)
        keys = jnp.concatenate([ref[:, columns(kv_head)] for ref in block_refs], axis=0)
        values = jnp.concatenate(
            [ref[:, columns(kv_heads + kv_head)] for ref in block_refs], axis=0
        )
        values = jnp.concatenate([values, jnp.ones_like(values)], axis=1)
        queries = []
        for head in heads:
            query = query_ref[:, columns(head)]
            if first:
                raw = query.astype(jnp.float32)
                mean = jnp.mean(raw * raw, axis=-1, keepdims=True)
                query = (raw * lax.rsqrt(mean + EPS) * gain_ref[...]).astype(jnp.bfloat16)
                normed_ref[:, columns(head)] = query
            queries.append(query)
        scores = lax.dot_general(
            jnp.concatenate(queries, axis=0),
            keys,
            (((1,), (1,)), ((), ())),
            preferred_element_type=jnp.float32,
        )
        weights = (jnp.exp2(scores) * is_open).astype(jnp.bfloat16)
        both = jnp.dot(weights, values, preferred_element_type=jnp.float32)
        for at, head in enumerate(heads):
            sums = both[at * rows : (at + 1) * rows, :HEAD_SIZE]
            total = both[at * rows : (at + 1) * rows, HEAD_SIZE:]
            if not first:
                sums = sums + sums_in[:, columns(head)]
                total = total + totals_in[:, head : head + 1]
            if last:
                safe = jnp.where(total > 0, total, jnp.ones_like(total))
                inverse = pl.reciprocal(safe, approx=True)
                inverse = inverse * (2.0 - safe * inverse)
                refs[0][:, columns(head)] = (sums * inverse).astype(jnp.bfloat16)
            else:
                refs[0][:, columns(head)] = sums
                totals = jnp.where(lane == head, total, totals)
    if not last:
        refs[1][...] = totals


def attend_cost(rows, width, keys):
    return pl.CostEstimate(
        flops=16 * rows * width * keys,
        transcendentals=rows * width // HEAD_SIZE * keys,
        bytes_accessed=2 * rows * width,
    )


def attend(query, blocks, is_open, gain, carried, last, name):
    first = carried is None
    rows, width = query.shape
    kv_heads = blocks[0].shape[1] // (2 * HEAD_SIZE)
    operands = [query, *blocks, is_open] + ([gain] if first else list(carried))
    if last:
        out_shape = [jax.ShapeDtypeStruct((rows, width), jnp.bfloat16)]
    else:
        out_shape = [
            jax.ShapeDtypeStruct((rows, width), jnp.float32),
            jax.ShapeDtypeStruct((rows, HEAD_SIZE), jnp.float32),
        ]
    if first:
        out_shape.insert(0, jax.ShapeDtypeStruct((rows, width), jnp.bfloat16))
    return pl.pallas_call(
        functools.partial(attend_kernel, first, last, kv_heads),
        out_shape=out_shape,
        in_specs=[WHOLE] * len(operands),
        out_specs=[WHOLE] * len(out_shape),
        cost_estimate=attend_cost(rows, width, REACH * blocks[0].shape[0]),
        compiler_params=pltpu.CompilerParams(vmem_limit_bytes=ATTEND_VMEM),
        name=name,
    )(*operands)


def after(values, *others):
    return lax.optimization_barrier((values, others))[0]


def body(
    text_query_matrix, vision, key_matrix, value_matrix, query_norm_gain, key_gain, block_mask
):
    position = lax.axis_index("seq")
    images = lax.broadcasted_iota(jnp.int32, (1, block_mask.shape[1], REACH), 1)
    wanted = position - lax.broadcasted_iota(jnp.int32, (1, block_mask.shape[1], REACH), 2)
    is_open = jnp.sum(jnp.where(images == wanted, block_mask[:, :, None], 0), axis=1)
    is_open = jnp.repeat(is_open.astype(jnp.float32), BLOCK, axis=0)
    query_gain = (query_norm_gain * SCORE_SCALE).reshape(1, HEAD_SIZE)
    key_gain = key_gain.reshape(1, HEAD_SIZE)

    def projected(row_parts, name):
        return project(row_parts, key_matrix, value_matrix, key_gain, "project_" + name)

    def reached(block):
        return [block] + [shifted(block, "seq", by) for by in range(1, REACH)]

    left = turned(vision, "tp", 1)
    right = turned(vision, "tp", -1)
    own = projected([vision], "own")
    own_blocks = reached(own)
    normed, *carried = attend(
        text_query_matrix, own_blocks, is_open, query_gain, None, False, "attend_own"
    )

    half = vision.shape[0] // 2
    left, right = after((left, right), carried)
    upper_across = turned(left[:half], "tp", 1)
    lower_across = turned(right[half:], "tp", -1)
    sides = projected([left, right], "sides")
    side_blocks = reached(sides)
    upper_across, lower_across = after((upper_across, lower_across), sides)
    across = projected([upper_across, lower_across], "across")
    across_blocks = reached(across)
    side_blocks = after(side_blocks, across)
    carried = attend(normed, side_blocks, is_open, None, carried, False, "attend_sides")
    across_blocks = after(across_blocks, carried)
    (result,) = attend(normed, across_blocks, is_open, None, carried, True, "attend_across")
    return result


def solution(mesh):
    placed = (
        P("seq", "tp"),
        P(("seq", "tp"), None),
        P(None, "tp"),
        P(None, "tp"),
        P(),
        P(),
        P("seq", None),
    )
    return jax.shard_map(
        body, mesh=mesh, in_specs=placed, out_specs=P("seq", "tp"), check_vma=False
    )
```

```python
import functools
import math

import jax
import jax.numpy as jnp
from jax import lax
from jax.experimental import pallas as pl
from jax.experimental.pallas import tpu as pltpu
from jax.sharding import PartitionSpec as P

HEAD_SIZE = 128
REACH = 4
BLOCK = 64
EPS = 1e-05
SCORE_SCALE = HEAD_SIZE ** (-0.5) * math.log2(math.e)
PROJECT_VMEM = 8 * 1024 * 1024
ATTEND_VMEM = 20 * 1024 * 1024
WHOLE = pl.BlockSpec(memory_space=pltpu.VMEM)


def turned(value, axis, by):
    length = lax.axis_size(axis)
    return lax.ppermute(value, axis, [(i, (i + by) % length) for i in range(length)])


def project_rows(row_refs, key_ref, value_ref, gain_ref, out_ref):
    width = key_ref.shape[1]
    rows = [ref[...] for ref in row_refs]
    rows = rows[0] if len(rows) == 1 else jnp.concatenate(rows, axis=0)
    keys = jnp.dot(rows, key_ref[...], preferred_element_type=jnp.float32)
    values = jnp.dot(rows, value_ref[...], preferred_element_type=jnp.float32)
    for head in range(width // HEAD_SIZE):
        at = slice(head * HEAD_SIZE, (head + 1) * HEAD_SIZE)
        own = keys[:, at]
        mean = jnp.mean(own * own, axis=-1, keepdims=True)
        out_ref[:, at] = (own * lax.rsqrt(mean + EPS) * gain_ref[...]).astype(out_ref.dtype)
    out_ref[:, width:] = values.astype(out_ref.dtype)


def project_cost(rows, key_matrix):
    size = math.prod(key_matrix.shape)
    return pl.CostEstimate(flops=4 * rows * size, transcendentals=0, bytes_accessed=4 * size)


def project_kernel(*refs):
    *row_refs, key_ref, value_ref, gain_ref, out_ref = refs
    project_rows(row_refs, key_ref, value_ref, gain_ref, out_ref)


def project(row_parts, key_matrix, value_matrix, key_gain, name):
    width = key_matrix.shape[1]
    rows = sum(each.shape[0] for each in row_parts)
    return pl.pallas_call(
        project_kernel,
        out_shape=jax.ShapeDtypeStruct((rows, 2 * width), jnp.bfloat16),
        in_specs=[WHOLE] * (len(row_parts) + 3),
        out_specs=WHOLE,
        cost_estimate=project_cost(rows, key_matrix),
        compiler_params=pltpu.CompilerParams(vmem_limit_bytes=PROJECT_VMEM),
        name=name,
    )(*row_parts, key_matrix, value_matrix, key_gain)


def attend_kernel(first, last, kv_heads, *refs):
    refs = list(refs)
    query_ref = refs.pop(0)
    block_refs = [refs.pop(0) for _ in range(REACH)]
    open_ref = refs.pop(0)
    if first:
        gain_ref, normed_ref = refs.pop(0), refs.pop(0)
    else:
        sums_in, totals_in = refs.pop(0), refs.pop(0)
    rows = query_ref.shape[0]
    count = block_refs[0].shape[0]
    group = query_ref.shape[1] // HEAD_SIZE // kv_heads
    image = lax.broadcasted_iota(jnp.int32, (rows, REACH * count), 1) // count
    is_open = jnp.zeros((rows, REACH * count), jnp.float32)
    for at in range(REACH):
        is_open = jnp.where(image == at, open_ref[:, at : at + 1], is_open)
    is_open = jnp.concatenate([is_open] * group, axis=0)
    lane = lax.broadcasted_iota(jnp.int32, (rows, HEAD_SIZE), 1)
    totals = jnp.zeros((rows, HEAD_SIZE), jnp.float32)

    def columns(head):
        return slice(head * HEAD_SIZE, (head + 1) * HEAD_SIZE)

    for kv_head in range(kv_heads):
        heads = range(kv_head * group, (kv_head + 1) * group)
        keys = jnp.concatenate([ref[:, columns(kv_head)] for ref in block_refs], axis=0)
        values = jnp.concatenate(
            [ref[:, columns(kv_heads + kv_head)] for ref in block_refs], axis=0
        )
        values = jnp.concatenate([values, jnp.ones_like(values)], axis=1)
        queries = []
        for head in heads:
            query = query_ref[:, columns(head)]
            if first:
                raw = query.astype(jnp.float32)
                mean = jnp.mean(raw * raw, axis=-1, keepdims=True)
                query = (raw * lax.rsqrt(mean + EPS) * gain_ref[...]).astype(jnp.bfloat16)
                normed_ref[:, columns(head)] = query
            queries.append(query)
        scores = lax.dot_general(
            jnp.concatenate(queries, axis=0),
            keys,
            (((1,), (1,)), ((), ())),
            preferred_element_type=jnp.float32,
        )
        weights = (jnp.exp2(scores) * is_open).astype(jnp.bfloat16)
        both = jnp.dot(weights, values, preferred_element_type=jnp.float32)
        for at, head in enumerate(heads):
            sums = both[at * rows : (at + 1) * rows, :HEAD_SIZE]
            total = both[at * rows : (at + 1) * rows, HEAD_SIZE:]
            if not first:
                sums = sums + sums_in[:, columns(head)]
                total = total + totals_in[:, head : head + 1]
            if last:
                safe = jnp.where(total > 0, total, jnp.ones_like(total))
                inverse = pl.reciprocal(safe, approx=True)
                inverse = inverse * (2.0 - safe * inverse)
                refs[0][:, columns(head)] = (sums * inverse).astype(jnp.bfloat16)
            else:
                refs[0][:, columns(head)] = sums
                totals = jnp.where(lane == head, total, totals)
    if not last:
        refs[1][...] = totals


def attend_cost(rows, width, keys):
    return pl.CostEstimate(
        flops=16 * rows * width * keys,
        transcendentals=rows * width // HEAD_SIZE * keys,
        bytes_accessed=2 * rows * width,
    )


def attend(query, blocks, is_open, gain, carried, last, name):
    first = carried is None
    rows, width = query.shape
    kv_heads = blocks[0].shape[1] // (2 * HEAD_SIZE)
    operands = [query, *blocks, is_open] + ([gain] if first else list(carried))
    if last:
        out_shape = [jax.ShapeDtypeStruct((rows, width), jnp.bfloat16)]
    else:
        out_shape = [
            jax.ShapeDtypeStruct((rows, width), jnp.float32),
            jax.ShapeDtypeStruct((rows, HEAD_SIZE), jnp.float32),
        ]
    if first:
        out_shape.insert(0, jax.ShapeDtypeStruct((rows, width), jnp.bfloat16))
    return pl.pallas_call(
        functools.partial(attend_kernel, first, last, kv_heads),
        out_shape=out_shape,
        in_specs=[WHOLE] * len(operands),
        out_specs=[WHOLE] * len(out_shape),
        cost_estimate=attend_cost(rows, width, REACH * blocks[0].shape[0]),
        compiler_params=pltpu.CompilerParams(vmem_limit_bytes=ATTEND_VMEM),
        name=name,
    )(*operands)


def after(values, *others):
    return lax.optimization_barrier((values, others))[0]


def body(
    text_query_matrix, vision, key_matrix, value_matrix, query_norm_gain, key_gain, block_mask
):
    position = lax.axis_index("seq")
    images = lax.broadcasted_iota(jnp.int32, (1, block_mask.shape[1], REACH), 1)
    wanted = position - lax.broadcasted_iota(jnp.int32, (1, block_mask.shape[1], REACH), 2)
    is_open = jnp.sum(jnp.where(images == wanted, block_mask[:, :, None], 0), axis=1)
    is_open = jnp.repeat(is_open.astype(jnp.float32), BLOCK, axis=0)
    query_gain = (query_norm_gain * SCORE_SCALE).reshape(1, HEAD_SIZE)
    key_gain = key_gain.reshape(1, HEAD_SIZE)

    def projected(row_parts, name):
        return project(row_parts, key_matrix, value_matrix, key_gain, "project_" + name)

    def reached(block):
        return [block] + [turned(block, "seq", by) for by in range(1, REACH)]

    left = turned(vision, "tp", 1)
    right = turned(vision, "tp", -1)
    own = projected([vision], "own")
    own_blocks = reached(own)
    normed, *carried = attend(
        text_query_matrix, own_blocks, is_open, query_gain, None, False, "attend_own"
    )

    half = vision.shape[0] // 2
    left, right = after((left, right), carried)
    upper_across = turned(left[:half], "tp", 1)
    lower_across = turned(right[half:], "tp", -1)
    sides = projected([left, right], "sides")
    side_blocks = reached(sides)
    upper_across, lower_across = after((upper_across, lower_across), sides)
    across = projected([upper_across, lower_across], "across")
    across_blocks = reached(across)
    side_blocks = after(side_blocks, across)
    carried = attend(normed, side_blocks, is_open, None, carried, False, "attend_sides")
    across_blocks = after(across_blocks, carried)
    (result,) = attend(normed, across_blocks, is_open, None, carried, True, "attend_across")
    return result


def solution(mesh):
    placed = (
        P("seq", "tp"),
        P(("seq", "tp"), None),
        P(None, "tp"),
        P(None, "tp"),
        P(),
        P(),
        P("seq", None),
    )
    return jax.shard_map(
        body, mesh=mesh, in_specs=placed, out_specs=P("seq", "tp"), check_vma=False
    )
```

```python
import functools
import math

import jax
import jax.numpy as jnp
from jax import lax
from jax.experimental import pallas as pl
from jax.experimental.pallas import tpu as pltpu
from jax.sharding import PartitionSpec as P

HEAD_SIZE = 128
REACH = 4
BLOCK = 64
EPS = 1e-05
SCORE_SCALE = HEAD_SIZE ** (-0.5) * math.log2(math.e)
PROJECT_VMEM = 8 * 1024 * 1024
ATTEND_VMEM = 20 * 1024 * 1024
WHOLE = pl.BlockSpec(memory_space=pltpu.VMEM)


def turned(value, axis, by):
    length = lax.axis_size(axis)
    return lax.ppermute(value, axis, [(i, (i + by) % length) for i in range(length)])


def project_rows(row_refs, key_ref, value_ref, gain_ref, out_ref):
    width = key_ref.shape[1]
    rows = [ref[...] for ref in row_refs]
    rows = rows[0] if len(rows) == 1 else jnp.concatenate(rows, axis=0)
    keys = jnp.dot(rows, key_ref[...], preferred_element_type=jnp.float32)
    values = jnp.dot(rows, value_ref[...], preferred_element_type=jnp.float32)
    for head in range(width // HEAD_SIZE):
        at = slice(head * HEAD_SIZE, (head + 1) * HEAD_SIZE)
        own = keys[:, at]
        mean = jnp.mean(own * own, axis=-1, keepdims=True)
        out_ref[:, at] = (own * lax.rsqrt(mean + EPS) * gain_ref[...]).astype(out_ref.dtype)
    out_ref[:, width:] = values.astype(out_ref.dtype)


def project_cost(rows, key_matrix):
    size = math.prod(key_matrix.shape)
    return pl.CostEstimate(flops=4 * rows * size, transcendentals=0, bytes_accessed=4 * size)


def project_kernel(*refs):
    *row_refs, key_ref, value_ref, gain_ref, out_ref = refs
    project_rows(row_refs, key_ref, value_ref, gain_ref, out_ref)


def project(row_parts, key_matrix, value_matrix, key_gain, name):
    width = key_matrix.shape[1]
    rows = sum(each.shape[0] for each in row_parts)
    return pl.pallas_call(
        project_kernel,
        out_shape=jax.ShapeDtypeStruct((rows, 2 * width), jnp.bfloat16),
        in_specs=[WHOLE] * (len(row_parts) + 3),
        out_specs=WHOLE,
        cost_estimate=project_cost(rows, key_matrix),
        compiler_params=pltpu.CompilerParams(vmem_limit_bytes=PROJECT_VMEM),
        name=name,
    )(*row_parts, key_matrix, value_matrix, key_gain)


def attend_kernel(first, last, kv_heads, *refs):
    refs = list(refs)
    query_ref = refs.pop(0)
    block_refs = [refs.pop(0) for _ in range(REACH)]
    open_ref = refs.pop(0)
    if first:
        gain_ref, normed_ref = refs.pop(0), refs.pop(0)
    else:
        sums_in, totals_in = refs.pop(0), refs.pop(0)
    rows = query_ref.shape[0]
    count = block_refs[0].shape[0]
    group = query_ref.shape[1] // HEAD_SIZE // kv_heads
    image = lax.broadcasted_iota(jnp.int32, (rows, REACH * count), 1) // count
    is_open = jnp.zeros((rows, REACH * count), jnp.float32)
    for at in range(REACH):
        is_open = jnp.where(image == at, open_ref[:, at : at + 1], is_open)
    is_open = jnp.concatenate([is_open] * group, axis=0)
    lane = lax.broadcasted_iota(jnp.int32, (rows, HEAD_SIZE), 1)
    totals = jnp.zeros((rows, HEAD_SIZE), jnp.float32)

    def columns(head):
        return slice(head * HEAD_SIZE, (head + 1) * HEAD_SIZE)

    for kv_head in range(kv_heads):
        heads = range(kv_head * group, (kv_head + 1) * group)
        keys = jnp.concatenate([ref[:, columns(kv_head)] for ref in block_refs], axis=0)
        values = jnp.concatenate(
            [ref[:, columns(kv_heads + kv_head)] for ref in block_refs], axis=0
        )
        values = jnp.concatenate([values, jnp.ones_like(values)], axis=1)
        queries = []
        for head in heads:
            query = query_ref[:, columns(head)]
            if first:
                raw = query.astype(jnp.float32)
                mean = jnp.mean(raw * raw, axis=-1, keepdims=True)
                query = (raw * lax.rsqrt(mean + EPS) * gain_ref[...]).astype(jnp.bfloat16)
                normed_ref[:, columns(head)] = query
            queries.append(query)
        scores = lax.dot_general(
            jnp.concatenate(queries, axis=0),
            keys,
            (((1,), (1,)), ((), ())),
            preferred_element_type=jnp.float32,
        )
        weights = (jnp.exp2(scores) * is_open).astype(jnp.bfloat16)
        both = jnp.dot(weights, values, preferred_element_type=jnp.float32)
        for at, head in enumerate(heads):
            sums = both[at * rows : (at + 1) * rows, :HEAD_SIZE]
            total = both[at * rows : (at + 1) * rows, HEAD_SIZE:]
            if not first:
                sums = sums + sums_in[:, columns(head)]
                total = total + totals_in[:, head : head + 1]
            if last:
                safe = jnp.where(total > 0, total, jnp.ones_like(total))
                inverse = pl.reciprocal(safe, approx=True)
                inverse = inverse * (2.0 - safe * inverse)
                refs[0][:, columns(head)] = (sums * inverse).astype(jnp.bfloat16)
            else:
                refs[0][:, columns(head)] = sums
                totals = jnp.where(lane == head, total, totals)
    if not last:
        refs[1][...] = totals


def attend_cost(rows, width, keys):
    return pl.CostEstimate(
        flops=12 * rows * width * keys,
        transcendentals=rows * width // HEAD_SIZE * keys,
        bytes_accessed=2 * rows * width,
    )


def attend(query, blocks, is_open, gain, carried, last, name):
    first = carried is None
    rows, width = query.shape
    kv_heads = blocks[0].shape[1] // (2 * HEAD_SIZE)
    operands = [query, *blocks, is_open] + ([gain] if first else list(carried))
    if last:
        out_shape = [jax.ShapeDtypeStruct((rows, width), jnp.bfloat16)]
    else:
        out_shape = [
            jax.ShapeDtypeStruct((rows, width), jnp.float32),
            jax.ShapeDtypeStruct((rows, HEAD_SIZE), jnp.float32),
        ]
    if first:
        out_shape.insert(0, jax.ShapeDtypeStruct((rows, width), jnp.bfloat16))
    return pl.pallas_call(
        functools.partial(attend_kernel, first, last, kv_heads),
        out_shape=out_shape,
        in_specs=[WHOLE] * len(operands),
        out_specs=[WHOLE] * len(out_shape),
        cost_estimate=attend_cost(rows, width, REACH * blocks[0].shape[0]),
        compiler_params=pltpu.CompilerParams(vmem_limit_bytes=ATTEND_VMEM),
        name=name,
    )(*operands)


def after(values, *others):
    return lax.optimization_barrier((values, others))[0]


def body(
    text_query_matrix, vision, key_matrix, value_matrix, query_norm_gain, key_gain, block_mask
):
    position = lax.axis_index("seq")
    images = lax.broadcasted_iota(jnp.int32, (1, block_mask.shape[1], REACH), 1)
    wanted = position - lax.broadcasted_iota(jnp.int32, (1, block_mask.shape[1], REACH), 2)
    is_open = jnp.sum(jnp.where(images == wanted, block_mask[:, :, None], 0), axis=1)
    is_open = jnp.repeat(is_open.astype(jnp.float32), BLOCK, axis=0)
    query_gain = (query_norm_gain * SCORE_SCALE).reshape(1, HEAD_SIZE)
    key_gain = key_gain.reshape(1, HEAD_SIZE)

    def projected(row_parts, name):
        return project(row_parts, key_matrix, value_matrix, key_gain, "project_" + name)

    def reached(block):
        return [block] + [turned(block, "seq", by) for by in range(1, REACH)]

    half = vision.shape[0] // 2
    upper = vision[:half]
    lower = after(vision, upper)[half:]
    upper_left = turned(upper, "tp", 1)
    lower_right = turned(lower, "tp", -1)
    lower_left = turned(lower, "tp", 1)
    upper_right = turned(upper, "tp", -1)

    own = projected([vision], "own")
    own_blocks = reached(own)
    upper_left, lower_right = after((upper_left, lower_right), own)
    upper_across = turned(upper_left, "tp", 1)
    lower_across = turned(lower_right, "tp", -1)
    normed, *carried = attend(
        text_query_matrix, own_blocks, is_open, query_gain, None, False, "attend_own"
    )

    lower_left, upper_right = after((lower_left, upper_right), carried)
    sides = projected([upper_left, lower_left, upper_right, lower_right], "sides")
    side_blocks = reached(sides)
    upper_across, lower_across = after((upper_across, lower_across), sides)
    across = projected([upper_across, lower_across], "across")
    across_blocks = reached(across)
    side_blocks = after(side_blocks, across)
    carried = attend(normed, side_blocks, is_open, None, carried, False, "attend_sides")
    across_blocks = after(across_blocks, carried)
    (result,) = attend(normed, across_blocks, is_open, None, carried, True, "attend_across")
    return result


def solution(mesh):
    placed = (
        P("seq", "tp"),
        P(("seq", "tp"), None),
        P(None, "tp"),
        P(None, "tp"),
        P(),
        P(),
        P("seq", None),
    )
    return jax.shard_map(
        body, mesh=mesh, in_specs=placed, out_specs=P("seq", "tp"), check_vma=False
    )
```

```python
import functools
import math

import jax
import jax.numpy as jnp
from jax import lax
from jax.experimental import pallas as pl
from jax.experimental.pallas import tpu as pltpu
from jax.sharding import PartitionSpec as P

HEAD_SIZE = 128
REACH = 4
BLOCK = 64
EPS = 1e-05
SCORE_SCALE = HEAD_SIZE ** (-0.5) * math.log2(math.e)
PROJECT_VMEM = 8 * 1024 * 1024
FETCH_PASSES = 4
ATTEND_VMEM = 20 * 1024 * 1024
WHOLE = pl.BlockSpec(memory_space=pltpu.VMEM)


def sent(value, axis, target):
    length = lax.axis_size(axis)
    return lax.ppermute(value, axis, [(i, target(i) % length) for i in range(length)])


def turned(value, axis, by):
    return sent(value, axis, lambda i: i + by)


def from_reach(block):
    across = sent(block, "seq", lambda s: s + 2)
    other = sent(block, "seq", lambda s: s + 1 + 2 * (s % 2))
    swapped = sent(across, "seq", lambda s: s + 1 - 2 * (s % 2))
    return [block, other, across, swapped]


def from_distances(position, at):
    near_far = jnp.where(position % 2 == 0, 3, 1)
    return jnp.where(at == 1, near_far, jnp.where(at == 3, 4 - near_far, at))


def project_rows(row_refs, key_ref, value_ref, gain_ref, out_ref):
    width = key_ref.shape[1]
    rows = [ref[...] for ref in row_refs]
    rows = rows[0] if len(rows) == 1 else jnp.concatenate(rows, axis=0)
    keys = jnp.dot(rows, key_ref[...], preferred_element_type=jnp.float32)
    values = jnp.dot(rows, value_ref[...], preferred_element_type=jnp.float32)
    for head in range(width // HEAD_SIZE):
        at = slice(head * HEAD_SIZE, (head + 1) * HEAD_SIZE)
        own = keys[:, at]
        mean = jnp.mean(own * own, axis=-1, keepdims=True)
        out_ref[:, at] = (own * lax.rsqrt(mean + EPS) * gain_ref[...]).astype(out_ref.dtype)
    out_ref[:, width:] = values.astype(out_ref.dtype)


def project_cost(rows, key_matrix):
    size = math.prod(key_matrix.shape)
    return pl.CostEstimate(flops=4 * rows * size, transcendentals=0, bytes_accessed=4 * size)


def project_kernel(*refs):
    *row_refs, key_ref, value_ref, gain_ref, out_ref = refs
    project_rows(row_refs, key_ref, value_ref, gain_ref, out_ref)


def project(row_parts, key_matrix, value_matrix, key_gain, name):
    width = key_matrix.shape[1]
    rows = sum(each.shape[0] for each in row_parts)
    return pl.pallas_call(
        project_kernel,
        out_shape=jax.ShapeDtypeStruct((rows, 2 * width), jnp.bfloat16),
        in_specs=[WHOLE] * (len(row_parts) + 3),
        out_specs=WHOLE,
        cost_estimate=project_cost(rows, key_matrix),
        compiler_params=pltpu.CompilerParams(vmem_limit_bytes=PROJECT_VMEM),
        name=name,
    )(*row_parts, key_matrix, value_matrix, key_gain)


def attend_kernel(first, last, kv_heads, *refs):
    refs = list(refs)
    query_ref = refs.pop(0)
    block_refs = [refs.pop(0) for _ in range(REACH)]
    open_ref = refs.pop(0)
    if first:
        gain_ref, normed_ref = refs.pop(0), refs.pop(0)
    else:
        sums_in, totals_in = refs.pop(0), refs.pop(0)
    rows = query_ref.shape[0]
    count = block_refs[0].shape[0]
    group = query_ref.shape[1] // HEAD_SIZE // kv_heads
    image = lax.broadcasted_iota(jnp.int32, (rows, REACH * count), 1) // count
    is_open = jnp.zeros((rows, REACH * count), jnp.float32)
    for at in range(REACH):
        is_open = jnp.where(image == at, open_ref[:, at : at + 1], is_open)
    is_open = jnp.concatenate([is_open] * group, axis=0)
    lane = lax.broadcasted_iota(jnp.int32, (rows, HEAD_SIZE), 1)
    totals = jnp.zeros((rows, HEAD_SIZE), jnp.float32)

    def columns(head):
        return slice(head * HEAD_SIZE, (head + 1) * HEAD_SIZE)

    for kv_head in range(kv_heads):
        heads = range(kv_head * group, (kv_head + 1) * group)
        keys = jnp.concatenate([ref[:, columns(kv_head)] for ref in block_refs], axis=0)
        values = jnp.concatenate(
            [ref[:, columns(kv_heads + kv_head)] for ref in block_refs], axis=0
        )
        values = jnp.concatenate([values, jnp.ones_like(values)], axis=1)
        queries = []
        for head in heads:
            query = query_ref[:, columns(head)]
            if first:
                raw = query.astype(jnp.float32)
                mean = jnp.mean(raw * raw, axis=-1, keepdims=True)
                query = (raw * lax.rsqrt(mean + EPS) * gain_ref[...]).astype(jnp.bfloat16)
                normed_ref[:, columns(head)] = query
            queries.append(query)
        scores = lax.dot_general(
            jnp.concatenate(queries, axis=0),
            keys,
            (((1,), (1,)), ((), ())),
            preferred_element_type=jnp.float32,
        )
        weights = (jnp.exp2(scores) * is_open).astype(jnp.bfloat16)
        both = jnp.dot(weights, values, preferred_element_type=jnp.float32)
        for at, head in enumerate(heads):
            sums = both[at * rows : (at + 1) * rows, :HEAD_SIZE]
            total = both[at * rows : (at + 1) * rows, HEAD_SIZE:]
            if not first:
                sums = sums + sums_in[:, columns(head)]
                total = total + totals_in[:, head : head + 1]
            if last:
                safe = jnp.where(total > 0, total, jnp.ones_like(total))
                inverse = pl.reciprocal(safe, approx=True)
                inverse = inverse * (2.0 - safe * inverse)
                refs[0][:, columns(head)] = (sums * inverse).astype(jnp.bfloat16)
            else:
                refs[0][:, columns(head)] = sums
                totals = jnp.where(lane == head, total, totals)
    if not last:
        refs[1][...] = totals


def attend_cost(rows, width, keys, passes):
    return pl.CostEstimate(
        flops=4 * passes * rows * width * keys,
        transcendentals=rows * width // HEAD_SIZE * keys,
        bytes_accessed=2 * rows * width,
    )


def attend(query, blocks, is_open, gain, carried, last, name):
    first = carried is None
    rows, width = query.shape
    kv_heads = blocks[0].shape[1] // (2 * HEAD_SIZE)
    operands = [query, *blocks, is_open] + ([gain] if first else list(carried))
    if last:
        out_shape = [jax.ShapeDtypeStruct((rows, width), jnp.bfloat16)]
    else:
        out_shape = [
            jax.ShapeDtypeStruct((rows, width), jnp.float32),
            jax.ShapeDtypeStruct((rows, HEAD_SIZE), jnp.float32),
        ]
    if first:
        out_shape.insert(0, jax.ShapeDtypeStruct((rows, width), jnp.bfloat16))
    return pl.pallas_call(
        functools.partial(attend_kernel, first, last, kv_heads),
        out_shape=out_shape,
        in_specs=[WHOLE] * len(operands),
        out_specs=[WHOLE] * len(out_shape),
        cost_estimate=attend_cost(rows, width, REACH * blocks[0].shape[0], FETCH_PASSES if first else 1),
        compiler_params=pltpu.CompilerParams(vmem_limit_bytes=ATTEND_VMEM),
        name=name,
    )(*operands)


def after(values, *others):
    return lax.optimization_barrier((values, others))[0]


def body(
    text_query_matrix, vision, key_matrix, value_matrix, query_norm_gain, key_gain, block_mask
):
    position = lax.axis_index("seq")
    images = lax.broadcasted_iota(jnp.int32, (1, block_mask.shape[1], REACH), 1)
    at = lax.broadcasted_iota(jnp.int32, (1, block_mask.shape[1], REACH), 2)
    wanted = position - from_distances(position, at)
    is_open = jnp.sum(jnp.where(images == wanted, block_mask[:, :, None], 0), axis=1)
    is_open = jnp.repeat(is_open.astype(jnp.float32), BLOCK, axis=0)
    query_gain = (query_norm_gain * SCORE_SCALE).reshape(1, HEAD_SIZE)
    key_gain = key_gain.reshape(1, HEAD_SIZE)

    def projected(row_parts, name):
        return project(row_parts, key_matrix, value_matrix, key_gain, "project_" + name)

    left = turned(vision, "tp", 1)
    right = turned(vision, "tp", -1)
    own = projected([vision], "own")
    own_blocks = from_reach(own)
    normed, *carried = attend(
        text_query_matrix, own_blocks, is_open, query_gain, None, False, "attend_own"
    )

    half = vision.shape[0] // 2
    left, right = after((left, right), carried)
    upper_across = turned(left[:half], "tp", 1)
    lower_across = turned(right[half:], "tp", -1)
    sides = projected([left, right], "sides")
    side_blocks = from_reach(sides)
    carried = attend(normed, side_blocks, is_open, None, carried, False, "attend_sides")
    upper_across, lower_across = after((upper_across, lower_across), carried)
    across = projected([upper_across, lower_across], "across")
    across_blocks = from_reach(across)
    (result,) = attend(normed, across_blocks, is_open, None, carried, True, "attend_across")
    return result


def solution(mesh):
    placed = (
        P("seq", "tp"),
        P(("seq", "tp"), None),
        P(None, "tp"),
        P(None, "tp"),
        P(),
        P(),
        P("seq", None),
    )
    return jax.shard_map(
        body, mesh=mesh, in_specs=placed, out_specs=P("seq", "tp"), check_vma=False
    )
```

```python
import functools
import math

import jax
import jax.numpy as jnp
from jax import lax
from jax.experimental import pallas as pl
from jax.experimental.pallas import tpu as pltpu
from jax.sharding import PartitionSpec as P

HEAD_SIZE = 128
REACH = 4
BLOCK = 64
EPS = 1e-05
SCORE_SCALE = HEAD_SIZE ** (-0.5) * math.log2(math.e)
PROJECT_VMEM = 8 * 1024 * 1024
FETCH_PASSES = 4
ATTEND_VMEM = 20 * 1024 * 1024
WHOLE = pl.BlockSpec(memory_space=pltpu.VMEM)


def turned(value, axis, by):
    length = lax.axis_size(axis)
    return lax.ppermute(value, axis, [(i, (i + by) % length) for i in range(length)])


def moved(value, axis, target):
    length = lax.axis_size(axis)
    pairs = [(i, target(i)) for i in range(length) if target(i) < length]
    return lax.ppermute(value, axis, pairs)


def from_reach(block, between=lambda across: across):
    across = moved(block, "seq", lambda s: s + 2)
    other = moved(block, "seq", lambda s: s + 1 + 2 * (s % 2))
    swapped = moved(between(across), "seq", lambda s: s + 1 - 2 * (s % 2))
    return [block, other, across, swapped]


def from_distances(position, at):
    near_far = jnp.where(position % 2 == 0, 3, 1)
    return jnp.where(at == 1, near_far, jnp.where(at == 3, 4 - near_far, at))


def project_rows(row_refs, key_ref, value_ref, gain_ref, out_ref):
    width = key_ref.shape[1]
    rows = [ref[...] for ref in row_refs]
    rows = rows[0] if len(rows) == 1 else jnp.concatenate(rows, axis=0)
    keys = jnp.dot(rows, key_ref[...], preferred_element_type=jnp.float32)
    values = jnp.dot(rows, value_ref[...], preferred_element_type=jnp.float32)
    for head in range(width // HEAD_SIZE):
        at = slice(head * HEAD_SIZE, (head + 1) * HEAD_SIZE)
        own = keys[:, at]
        mean = jnp.mean(own * own, axis=-1, keepdims=True)
        out_ref[:, at] = (own * lax.rsqrt(mean + EPS) * gain_ref[...]).astype(out_ref.dtype)
    out_ref[:, width:] = values.astype(out_ref.dtype)


def project_cost(rows, key_matrix):
    size = math.prod(key_matrix.shape)
    return pl.CostEstimate(flops=4 * rows * size, transcendentals=0, bytes_accessed=4 * size)


def project_kernel(*refs):
    *row_refs, key_ref, value_ref, gain_ref, out_ref = refs
    project_rows(row_refs, key_ref, value_ref, gain_ref, out_ref)


def project(row_parts, key_matrix, value_matrix, key_gain, name):
    width = key_matrix.shape[1]
    rows = sum(each.shape[0] for each in row_parts)
    return pl.pallas_call(
        project_kernel,
        out_shape=jax.ShapeDtypeStruct((rows, 2 * width), jnp.bfloat16),
        in_specs=[WHOLE] * (len(row_parts) + 3),
        out_specs=WHOLE,
        cost_estimate=project_cost(rows, key_matrix),
        compiler_params=pltpu.CompilerParams(vmem_limit_bytes=PROJECT_VMEM),
        name=name,
    )(*row_parts, key_matrix, value_matrix, key_gain)


def attend_kernel(first, last, kv_heads, *refs):
    refs = list(refs)
    query_ref = refs.pop(0)
    block_refs = [refs.pop(0) for _ in range(REACH)]
    open_ref = refs.pop(0)
    if first:
        gain_ref, normed_ref = refs.pop(0), refs.pop(0)
    else:
        sums_in, totals_in = refs.pop(0), refs.pop(0)
    rows = query_ref.shape[0]
    count = block_refs[0].shape[0]
    group = query_ref.shape[1] // HEAD_SIZE // kv_heads
    image = lax.broadcasted_iota(jnp.int32, (rows, REACH * count), 1) // count
    is_open = jnp.zeros((rows, REACH * count), jnp.float32)
    for at in range(REACH):
        is_open = jnp.where(image == at, open_ref[:, at : at + 1], is_open)
    is_open = jnp.concatenate([is_open] * group, axis=0)
    lane = lax.broadcasted_iota(jnp.int32, (rows, HEAD_SIZE), 1)
    totals = jnp.zeros((rows, HEAD_SIZE), jnp.float32)

    def columns(head):
        return slice(head * HEAD_SIZE, (head + 1) * HEAD_SIZE)

    for kv_head in range(kv_heads):
        heads = range(kv_head * group, (kv_head + 1) * group)
        keys = jnp.concatenate([ref[:, columns(kv_head)] for ref in block_refs], axis=0)
        values = jnp.concatenate(
            [ref[:, columns(kv_heads + kv_head)] for ref in block_refs], axis=0
        )
        values = jnp.concatenate([values, jnp.ones_like(values)], axis=1)
        queries = []
        for head in heads:
            query = query_ref[:, columns(head)]
            if first:
                raw = query.astype(jnp.float32)
                mean = jnp.mean(raw * raw, axis=-1, keepdims=True)
                query = (raw * lax.rsqrt(mean + EPS) * gain_ref[...]).astype(jnp.bfloat16)
                normed_ref[:, columns(head)] = query
            queries.append(query)
        scores = lax.dot_general(
            jnp.concatenate(queries, axis=0),
            keys,
            (((1,), (1,)), ((), ())),
            preferred_element_type=jnp.float32,
        )
        weights = (jnp.exp2(scores) * is_open).astype(jnp.bfloat16)
        both = jnp.dot(weights, values, preferred_element_type=jnp.float32)
        for at, head in enumerate(heads):
            sums = both[at * rows : (at + 1) * rows, :HEAD_SIZE]
            total = both[at * rows : (at + 1) * rows, HEAD_SIZE:]
            if not first:
                sums = sums + sums_in[:, columns(head)]
                total = total + totals_in[:, head : head + 1]
            if last:
                safe = jnp.where(total > 0, total, jnp.ones_like(total))
                inverse = pl.reciprocal(safe, approx=True)
                inverse = inverse * (2.0 - safe * inverse)
                refs[0][:, columns(head)] = (sums * inverse).astype(jnp.bfloat16)
            else:
                refs[0][:, columns(head)] = sums
                totals = jnp.where(lane == head, total, totals)
    if not last:
        refs[1][...] = totals


def attend_cost(rows, width, keys, passes):
    return pl.CostEstimate(
        flops=4 * passes * rows * width * keys,
        transcendentals=rows * width // HEAD_SIZE * keys,
        bytes_accessed=2 * rows * width,
    )


def attend(query, blocks, is_open, gain, carried, last, name):
    first = carried is None
    rows, width = query.shape
    kv_heads = blocks[0].shape[1] // (2 * HEAD_SIZE)
    operands = [query, *blocks, is_open] + ([gain] if first else list(carried))
    if last:
        out_shape = [jax.ShapeDtypeStruct((rows, width), jnp.bfloat16)]
    else:
        out_shape = [
            jax.ShapeDtypeStruct((rows, width), jnp.float32),
            jax.ShapeDtypeStruct((rows, HEAD_SIZE), jnp.float32),
        ]
    if first:
        out_shape.insert(0, jax.ShapeDtypeStruct((rows, width), jnp.bfloat16))
    return pl.pallas_call(
        functools.partial(attend_kernel, first, last, kv_heads),
        out_shape=out_shape,
        in_specs=[WHOLE] * len(operands),
        out_specs=[WHOLE] * len(out_shape),
        cost_estimate=attend_cost(rows, width, REACH * blocks[0].shape[0], FETCH_PASSES if first else 1),
        compiler_params=pltpu.CompilerParams(vmem_limit_bytes=ATTEND_VMEM),
        name=name,
    )(*operands)


def after(values, *others):
    return lax.optimization_barrier((values, others))[0]


def body(
    text_query_matrix, vision, key_matrix, value_matrix, query_norm_gain, key_gain, block_mask
):
    position = lax.axis_index("seq")
    images = lax.broadcasted_iota(jnp.int32, (1, block_mask.shape[1], REACH), 1)
    at = lax.broadcasted_iota(jnp.int32, (1, block_mask.shape[1], REACH), 2)
    wanted = position - from_distances(position, at)
    is_open = jnp.sum(jnp.where(images == wanted, block_mask[:, :, None], 0), axis=1)
    is_open = jnp.repeat(is_open.astype(jnp.float32), BLOCK, axis=0)
    query_gain = (query_norm_gain * SCORE_SCALE).reshape(1, HEAD_SIZE)
    key_gain = key_gain.reshape(1, HEAD_SIZE)

    def projected(row_parts, name):
        return project(row_parts, key_matrix, value_matrix, key_gain, "project_" + name)

    left = turned(vision, "tp", 1)
    right = turned(vision, "tp", -1)
    own = projected([vision], "own")
    own_blocks = from_reach(own)
    normed, *carried = attend(
        text_query_matrix, own_blocks, is_open, query_gain, None, False, "attend_own"
    )

    half = vision.shape[0] // 2
    left, right = after((left, right), carried)
    upper_across = turned(left[:half], "tp", 1)
    lower_across = turned(right[half:], "tp", -1)
    sides = projected([left, right], "sides")
    side_blocks = from_reach(sides)
    upper_across, lower_across = after((upper_across, lower_across), sides)
    across = projected([upper_across, lower_across], "across")
    side_blocks = after(side_blocks, across)
    carried = attend(normed, side_blocks, is_open, None, carried, False, "attend_sides")
    across_blocks = from_reach(across, lambda block: after(block, carried))
    (result,) = attend(normed, across_blocks, is_open, None, carried, True, "attend_across")
    return result


def solution(mesh):
    placed = (
        P("seq", "tp"),
        P(("seq", "tp"), None),
        P(None, "tp"),
        P(None, "tp"),
        P(),
        P(),
        P("seq", None),
    )
    return jax.shard_map(
        body, mesh=mesh, in_specs=placed, out_specs=P("seq", "tp"), check_vma=False
    )
```

```python
import functools
import math

import jax
import jax.numpy as jnp
from jax import lax
from jax.experimental import pallas as pl
from jax.experimental.pallas import tpu as pltpu
from jax.sharding import PartitionSpec as P

HEAD_SIZE = 128
REACH = 4
BLOCK = 64
EPS = 1e-05
SCORE_SCALE = HEAD_SIZE ** (-0.5) * math.log2(math.e)
PROJECT_VMEM = 8 * 1024 * 1024
ATTEND_VMEM = 20 * 1024 * 1024
WHOLE = pl.BlockSpec(memory_space=pltpu.VMEM)
IN_PLACE = pl.BlockSpec(memory_space=pl.ANY)
HEADS_OUT = 4


def turned(value, axis, by):
    length = lax.axis_size(axis)
    return lax.ppermute(value, axis, [(i, (i + by) % length) for i in range(length)])


def project_rows(row_refs, key_ref, value_ref, gain_ref, out_ref):
    width = key_ref.shape[1]
    rows = [ref[...] for ref in row_refs]
    rows = rows[0] if len(rows) == 1 else jnp.concatenate(rows, axis=0)
    keys = jnp.dot(rows, key_ref[...], preferred_element_type=jnp.float32)
    values = jnp.dot(rows, value_ref[...], preferred_element_type=jnp.float32)
    for head in range(width // HEAD_SIZE):
        at = slice(head * HEAD_SIZE, (head + 1) * HEAD_SIZE)
        own = keys[:, at]
        mean = jnp.mean(own * own, axis=-1, keepdims=True)
        out_ref[:, at] = (own * lax.rsqrt(mean + EPS) * gain_ref[...]).astype(out_ref.dtype)
    out_ref[:, width:] = values.astype(out_ref.dtype)


def project_cost(rows, key_matrix):
    size = math.prod(key_matrix.shape)
    return pl.CostEstimate(flops=4 * rows * size, transcendentals=0, bytes_accessed=4 * size)


def project_kernel(*refs):
    *row_refs, key_ref, value_ref, gain_ref, out_ref = refs
    project_rows(row_refs, key_ref, value_ref, gain_ref, out_ref)


def project(row_parts, key_matrix, value_matrix, key_gain, name):
    width = key_matrix.shape[1]
    rows = sum(each.shape[0] for each in row_parts)
    return pl.pallas_call(
        project_kernel,
        out_shape=jax.ShapeDtypeStruct((rows, 2 * width), jnp.bfloat16),
        in_specs=[WHOLE] * (len(row_parts) + 3),
        out_specs=WHOLE,
        cost_estimate=project_cost(rows, key_matrix),
        compiler_params=pltpu.CompilerParams(vmem_limit_bytes=PROJECT_VMEM),
        name=name,
    )(*row_parts, key_matrix, value_matrix, key_gain)


def attend_kernel(first, last, kv_heads, *refs):
    refs = list(refs)
    copies = []
    if last:
        sems, held = refs.pop(), refs.pop()
    query_ref = refs.pop(0)
    block_refs = [refs.pop(0) for _ in range(REACH)]
    open_ref = refs.pop(0)
    if first:
        gain_ref, normed_ref = refs.pop(0), refs.pop(0)
    else:
        sums_in, totals_in = refs.pop(0), refs.pop(0)
    rows = query_ref.shape[0]
    count = block_refs[0].shape[0]
    group = query_ref.shape[1] // HEAD_SIZE // kv_heads
    image = lax.broadcasted_iota(jnp.int32, (rows, REACH * count), 1) // count
    is_open = jnp.zeros((rows, REACH * count), jnp.float32)
    for at in range(REACH):
        is_open = jnp.where(image == at, open_ref[:, at : at + 1], is_open)
    is_open = jnp.concatenate([is_open] * group, axis=0)
    lane = lax.broadcasted_iota(jnp.int32, (rows, HEAD_SIZE), 1)
    totals = jnp.zeros((rows, HEAD_SIZE), jnp.float32)

    def columns(head):
        return slice(head * HEAD_SIZE, (head + 1) * HEAD_SIZE)

    for kv_head in range(kv_heads):
        heads = range(kv_head * group, (kv_head + 1) * group)
        keys = jnp.concatenate([ref[:, columns(kv_head)] for ref in block_refs], axis=0)
        values = jnp.concatenate(
            [ref[:, columns(kv_heads + kv_head)] for ref in block_refs], axis=0
        )
        values = jnp.concatenate([values, jnp.ones_like(values)], axis=1)
        queries = []
        for head in heads:
            query = query_ref[:, columns(head)]
            if first:
                raw = query.astype(jnp.float32)
                mean = jnp.mean(raw * raw, axis=-1, keepdims=True)
                query = (raw * lax.rsqrt(mean + EPS) * gain_ref[...]).astype(jnp.bfloat16)
                normed_ref[:, columns(head)] = query
            queries.append(query)
        scores = lax.dot_general(
            jnp.concatenate(queries, axis=0),
            keys,
            (((1,), (1,)), ((), ())),
            preferred_element_type=jnp.float32,
        )
        weights = (jnp.exp2(scores) * is_open).astype(jnp.bfloat16)
        both = jnp.dot(weights, values, preferred_element_type=jnp.float32)
        for at, head in enumerate(heads):
            sums = both[at * rows : (at + 1) * rows, :HEAD_SIZE]
            total = both[at * rows : (at + 1) * rows, HEAD_SIZE:]
            if not first:
                sums = sums + sums_in[:, columns(head)]
                total = total + totals_in[:, head : head + 1]
            if last:
                safe = jnp.where(total > 0, total, jnp.ones_like(total))
                inverse = pl.reciprocal(safe, approx=True)
                inverse = inverse * (2.0 - safe * inverse)
                held[:, columns(head)] = (sums * inverse).astype(jnp.bfloat16)
                if head % HEADS_OUT == HEADS_OUT - 1:
                    part = pl.ds((head + 1 - HEADS_OUT) * HEAD_SIZE, HEADS_OUT * HEAD_SIZE)
                    copies.append(
                        pltpu.make_async_copy(
                            held.at[:, part], refs[0].at[:, part], sems.at[head // HEADS_OUT]
                        )
                    )
                    copies[-1].start()
            else:
                refs[0][:, columns(head)] = sums
                totals = jnp.where(lane == head, total, totals)
    if not last:
        refs[1][...] = totals
    for copy in copies:
        copy.wait()


def attend_cost(rows, width, keys):
    return pl.CostEstimate(
        flops=16 * rows * width * keys,
        transcendentals=rows * width // HEAD_SIZE * keys,
        bytes_accessed=2 * rows * width,
    )


def attend(query, blocks, is_open, gain, carried, last, name):
    first = carried is None
    rows, width = query.shape
    kv_heads = blocks[0].shape[1] // (2 * HEAD_SIZE)
    operands = [query, *blocks, is_open] + ([gain] if first else list(carried))
    scratch_shapes = []
    if last:
        out_shape = [jax.ShapeDtypeStruct((rows, width), jnp.bfloat16)]
        scratch_shapes.append(pltpu.VMEM((rows, width), jnp.bfloat16))
        scratch_shapes.append(pltpu.SemaphoreType.DMA((width // (HEADS_OUT * HEAD_SIZE),)))
    else:
        out_shape = [
            jax.ShapeDtypeStruct((rows, width), jnp.float32),
            jax.ShapeDtypeStruct((rows, HEAD_SIZE), jnp.float32),
        ]
    if first:
        out_shape.insert(0, jax.ShapeDtypeStruct((rows, width), jnp.bfloat16))
    return pl.pallas_call(
        functools.partial(attend_kernel, first, last, kv_heads),
        out_shape=out_shape,
        in_specs=[WHOLE] * len(operands),
        out_specs=[IN_PLACE if last else WHOLE] * len(out_shape),
        scratch_shapes=scratch_shapes,
        cost_estimate=attend_cost(rows, width, REACH * blocks[0].shape[0]),
        compiler_params=pltpu.CompilerParams(vmem_limit_bytes=ATTEND_VMEM),
        name=name,
    )(*operands)


def after(values, *others):
    return lax.optimization_barrier((values, others))[0]


def body(
    text_query_matrix, vision, key_matrix, value_matrix, query_norm_gain, key_gain, block_mask
):
    position = lax.axis_index("seq")
    images = lax.broadcasted_iota(jnp.int32, (1, block_mask.shape[1], REACH), 1)
    wanted = position - lax.broadcasted_iota(jnp.int32, (1, block_mask.shape[1], REACH), 2)
    is_open = jnp.sum(jnp.where(images == wanted, block_mask[:, :, None], 0), axis=1)
    is_open = jnp.repeat(is_open.astype(jnp.float32), BLOCK, axis=0)
    query_gain = (query_norm_gain * SCORE_SCALE).reshape(1, HEAD_SIZE)
    key_gain = key_gain.reshape(1, HEAD_SIZE)

    def projected(row_parts, name):
        return project(row_parts, key_matrix, value_matrix, key_gain, "project_" + name)

    def reached(block):
        return [block] + [turned(block, "seq", by) for by in range(1, REACH)]

    left = turned(vision, "tp", 1)
    right = turned(vision, "tp", -1)
    own = projected([vision], "own")
    own_blocks = reached(own)
    normed, *carried = attend(
        text_query_matrix, own_blocks, is_open, query_gain, None, False, "attend_own"
    )

    half = vision.shape[0] // 2
    left, right = after((left, right), carried)
    upper_across = turned(left[:half], "tp", 1)
    lower_across = turned(right[half:], "tp", -1)
    sides = projected([left, right], "sides")
    side_blocks = reached(sides)
    upper_across, lower_across = after((upper_across, lower_across), sides)
    across = projected([upper_across, lower_across], "across")
    across_blocks = reached(across)
    side_blocks = after(side_blocks, across)
    carried = attend(normed, side_blocks, is_open, None, carried, False, "attend_sides")
    across_blocks = after(across_blocks, carried)
    (result,) = attend(normed, across_blocks, is_open, None, carried, True, "attend_across")
    return result


def solution(mesh):
    placed = (
        P("seq", "tp"),
        P(("seq", "tp"), None),
        P(None, "tp"),
        P(None, "tp"),
        P(),
        P(),
        P("seq", None),
    )
    return jax.shard_map(
        body, mesh=mesh, in_specs=placed, out_specs=P("seq", "tp"), check_vma=False
    )
```

```python
import functools
import math

import jax
import jax.numpy as jnp
from jax import lax
from jax.experimental import pallas as pl
from jax.experimental.pallas import tpu as pltpu
from jax.sharding import PartitionSpec as P

HEAD_SIZE = 128
REACH = 4
BLOCK = 64
EPS = 1e-05
SCORE_SCALE = HEAD_SIZE ** (-0.5) * math.log2(math.e)
PROJECT_VMEM = 8 * 1024 * 1024
ATTEND_VMEM = 20 * 1024 * 1024
WHOLE = pl.BlockSpec(memory_space=pltpu.VMEM)
IN_PLACE = pl.BlockSpec(memory_space=pl.ANY)
HEADS_OUT = 4


def turned(value, axis, by, wraps=True):
    length = lax.axis_size(axis)
    pairs = [(i, (i + by) % length) for i in range(length) if wraps or i + by < length]
    return lax.ppermute(value, axis, pairs)


def write_keys_values(keys, values, gain_ref, out_ref):
    width = keys.shape[1]
    for head in range(width // HEAD_SIZE):
        at = slice(head * HEAD_SIZE, (head + 1) * HEAD_SIZE)
        own = keys[:, at]
        mean = jnp.mean(own * own, axis=-1, keepdims=True)
        out_ref[:, at] = (own * lax.rsqrt(mean + EPS) * gain_ref[...]).astype(out_ref.dtype)
    out_ref[:, width:] = values.astype(out_ref.dtype)


def project_cost(rows, key_matrix):
    size = math.prod(key_matrix.shape)
    return pl.CostEstimate(flops=4 * rows * size, transcendentals=0, bytes_accessed=4 * size)


def project_kernel(*refs):
    *row_refs, key_ref, value_ref, gain_ref, out_ref = refs
    rows = [ref[...] for ref in row_refs]
    rows = rows[0] if len(rows) == 1 else jnp.concatenate(rows, axis=0)
    keys = jnp.dot(rows, key_ref[...], preferred_element_type=jnp.float32)
    values = jnp.dot(rows, value_ref[...], preferred_element_type=jnp.float32)
    write_keys_values(keys, values, gain_ref, out_ref)


def project(row_parts, key_matrix, value_matrix, key_gain, name):
    width = key_matrix.shape[1]
    rows = sum(each.shape[0] for each in row_parts)
    return pl.pallas_call(
        project_kernel,
        out_shape=jax.ShapeDtypeStruct((rows, 2 * width), jnp.bfloat16),
        in_specs=[WHOLE] * (len(row_parts) + 3),
        out_specs=WHOLE,
        cost_estimate=project_cost(rows, key_matrix),
        compiler_params=pltpu.CompilerParams(vmem_limit_bytes=PROJECT_VMEM),
        name=name,
    )(*row_parts, key_matrix, value_matrix, key_gain)


def first_columns_kernel(rows_ref, key_ref, value_ref, out_ref):
    depth, width = rows_ref.shape[1], key_ref.shape[1]
    rows = rows_ref[...]
    out_ref[:, :width] = jnp.dot(rows, key_ref[:depth], preferred_element_type=jnp.float32)
    out_ref[:, width:] = jnp.dot(rows, value_ref[:depth], preferred_element_type=jnp.float32)


def last_columns_kernel(rows_ref, sums_ref, key_ref, value_ref, gain_ref, out_ref):
    width = key_ref.shape[1]
    before = key_ref.shape[0] - rows_ref.shape[1]
    rows = rows_ref[...]
    keys = jnp.dot(rows, key_ref[before:], preferred_element_type=jnp.float32)
    values = jnp.dot(rows, value_ref[before:], preferred_element_type=jnp.float32)
    write_keys_values(
        sums_ref[:, :width] + keys, sums_ref[:, width:] + values, gain_ref, out_ref
    )


def project_by_columns(first_part, last_part, key_matrix, value_matrix, key_gain, name):
    rows, width = first_part.shape[0], key_matrix.shape[1]
    params = dict(
        out_specs=WHOLE,
        cost_estimate=project_cost(rows // 2, key_matrix),
        compiler_params=pltpu.CompilerParams(vmem_limit_bytes=PROJECT_VMEM),
    )
    sums = pl.pallas_call(
        first_columns_kernel,
        out_shape=jax.ShapeDtypeStruct((rows, 2 * width), jnp.float32),
        in_specs=[WHOLE] * 3,
        name=name + "_first",
        **params,
    )(first_part, key_matrix, value_matrix)
    last_part = after(last_part, sums)
    return pl.pallas_call(
        last_columns_kernel,
        out_shape=jax.ShapeDtypeStruct((rows, 2 * width), jnp.bfloat16),
        in_specs=[WHOLE] * 5,
        name=name + "_last",
        **params,
    )(last_part, sums, key_matrix, value_matrix, key_gain)


def attend_kernel(first, last, kv_heads, *refs):
    refs = list(refs)
    copies = []
    if last:
        sems, held = refs.pop(), refs.pop()
    query_ref = refs.pop(0)
    block_refs = [refs.pop(0) for _ in range(REACH)]
    open_ref = refs.pop(0)
    if first:
        gain_ref, normed_ref = refs.pop(0), refs.pop(0)
    else:
        sums_in, totals_in = refs.pop(0), refs.pop(0)
    rows = query_ref.shape[0]
    count = block_refs[0].shape[0]
    group = query_ref.shape[1] // HEAD_SIZE // kv_heads
    image = lax.broadcasted_iota(jnp.int32, (rows, REACH * count), 1) // count
    is_open = jnp.zeros((rows, REACH * count), jnp.float32)
    for at in range(REACH):
        is_open = jnp.where(image == at, open_ref[:, at : at + 1], is_open)
    is_open = jnp.concatenate([is_open] * group, axis=0)
    lane = lax.broadcasted_iota(jnp.int32, (rows, HEAD_SIZE), 1)
    totals = jnp.zeros((rows, HEAD_SIZE), jnp.float32)

    def columns(head):
        return slice(head * HEAD_SIZE, (head + 1) * HEAD_SIZE)

    for kv_head in range(kv_heads):
        heads = range(kv_head * group, (kv_head + 1) * group)
        keys = jnp.concatenate([ref[:, columns(kv_head)] for ref in block_refs], axis=0)
        values = jnp.concatenate(
            [ref[:, columns(kv_heads + kv_head)] for ref in block_refs], axis=0
        )
        values = jnp.concatenate([values, jnp.ones_like(values)], axis=1)
        queries = []
        for head in heads:
            query = query_ref[:, columns(head)]
            if first:
                raw = query.astype(jnp.float32)
                mean = jnp.mean(raw * raw, axis=-1, keepdims=True)
                query = (raw * lax.rsqrt(mean + EPS) * gain_ref[...]).astype(jnp.bfloat16)
                normed_ref[:, columns(head)] = query
            queries.append(query)
        scores = lax.dot_general(
            jnp.concatenate(queries, axis=0),
            keys,
            (((1,), (1,)), ((), ())),
            preferred_element_type=jnp.float32,
        )
        weights = (jnp.exp2(scores) * is_open).astype(jnp.bfloat16)
        both = jnp.dot(weights, values, preferred_element_type=jnp.float32)
        for at, head in enumerate(heads):
            sums = both[at * rows : (at + 1) * rows, :HEAD_SIZE]
            total = both[at * rows : (at + 1) * rows, HEAD_SIZE:]
            if not first:
                sums = sums + sums_in[:, columns(head)]
                total = total + totals_in[:, head : head + 1]
            if last:
                safe = jnp.where(total > 0, total, jnp.ones_like(total))
                inverse = pl.reciprocal(safe, approx=True)
                inverse = inverse * (2.0 - safe * inverse)
                held[:, columns(head)] = (sums * inverse).astype(jnp.bfloat16)
                if head % HEADS_OUT == HEADS_OUT - 1:
                    part = pl.ds((head + 1 - HEADS_OUT) * HEAD_SIZE, HEADS_OUT * HEAD_SIZE)
                    copies.append(
                        pltpu.make_async_copy(
                            held.at[:, part], refs[0].at[:, part], sems.at[head // HEADS_OUT]
                        )
                    )
                    copies[-1].start()
            else:
                refs[0][:, columns(head)] = sums
                totals = jnp.where(lane == head, total, totals)
    if not last:
        refs[1][...] = totals
    for copy in copies:
        copy.wait()


def attend_cost(rows, width, keys):
    return pl.CostEstimate(
        flops=16 * rows * width * keys,
        transcendentals=rows * width // HEAD_SIZE * keys,
        bytes_accessed=2 * rows * width,
    )


def attend(query, blocks, is_open, gain, carried, last, name):
    first = carried is None
    rows, width = query.shape
    kv_heads = blocks[0].shape[1] // (2 * HEAD_SIZE)
    operands = [query, *blocks, is_open] + ([gain] if first else list(carried))
    scratch_shapes = []
    if last:
        out_shape = [jax.ShapeDtypeStruct((rows, width), jnp.bfloat16)]
        scratch_shapes.append(pltpu.VMEM((rows, width), jnp.bfloat16))
        scratch_shapes.append(pltpu.SemaphoreType.DMA((width // (HEADS_OUT * HEAD_SIZE),)))
    else:
        out_shape = [
            jax.ShapeDtypeStruct((rows, width), jnp.float32),
            jax.ShapeDtypeStruct((rows, HEAD_SIZE), jnp.float32),
        ]
    if first:
        out_shape.insert(0, jax.ShapeDtypeStruct((rows, width), jnp.bfloat16))
    return pl.pallas_call(
        functools.partial(attend_kernel, first, last, kv_heads),
        out_shape=out_shape,
        in_specs=[WHOLE] * len(operands),
        out_specs=[IN_PLACE if last else WHOLE] * len(out_shape),
        scratch_shapes=scratch_shapes,
        cost_estimate=attend_cost(rows, width, REACH * blocks[0].shape[0]),
        compiler_params=pltpu.CompilerParams(vmem_limit_bytes=ATTEND_VMEM),
        name=name,
    )(*operands)


def after(values, *others):
    return lax.optimization_barrier((values, others))[0]


def body(
    text_query_matrix, vision, key_matrix, value_matrix, query_norm_gain, key_gain, block_mask
):
    position = lax.axis_index("seq")
    images = lax.broadcasted_iota(jnp.int32, (1, block_mask.shape[1], REACH), 1)
    wanted = position - lax.broadcasted_iota(jnp.int32, (1, block_mask.shape[1], REACH), 2)
    is_open = jnp.sum(jnp.where(images == wanted, block_mask[:, :, None], 0), axis=1)
    is_open = jnp.repeat(is_open.astype(jnp.float32), BLOCK, axis=0)
    query_gain = (query_norm_gain * SCORE_SCALE).reshape(1, HEAD_SIZE)
    key_gain = key_gain.reshape(1, HEAD_SIZE)

    def projected(row_parts, name):
        return project(row_parts, key_matrix, value_matrix, key_gain, "project_" + name)

    def reached(block, wraps=True):
        return [block] + [turned(block, "seq", by, wraps) for by in range(1, REACH)]

    left = turned(vision, "tp", 1)
    right = turned(vision, "tp", -1)
    own = projected([vision], "own")
    own_blocks = reached(own, wraps=False)
    normed, *carried = attend(
        text_query_matrix, own_blocks, is_open, query_gain, None, False, "attend_own"
    )

    half = vision.shape[1] // 2
    left, right = after((left, right), carried)
    first_across = turned(left[:, :half], "tp", 1)
    last_across = turned(right[:, half:], "tp", -1)
    sides = projected([left, right], "sides")
    side_blocks = reached(sides)
    first_across = after(first_across, sides)
    across = project_by_columns(
        first_across, last_across, key_matrix, value_matrix, key_gain, "project_across"
    )
    across_blocks = reached(across)
    side_blocks = after(side_blocks, across)
    carried = attend(normed, side_blocks, is_open, None, carried, False, "attend_sides")
    across_blocks = after(across_blocks, carried)
    (result,) = attend(normed, across_blocks, is_open, None, carried, True, "attend_across")
    return result


def solution(mesh):
    placed = (
        P("seq", "tp"),
        P(("seq", "tp"), None),
        P(None, "tp"),
        P(None, "tp"),
        P(),
        P(),
        P("seq", None),
    )
    return jax.shard_map(
        body, mesh=mesh, in_specs=placed, out_specs=P("seq", "tp"), check_vma=False
    )
```

```python
import functools
import math

import jax
import jax.numpy as jnp
from jax import lax
from jax.experimental import pallas as pl
from jax.experimental.pallas import tpu as pltpu
from jax.sharding import PartitionSpec as P

HEAD_SIZE = 128
REACH = 4
BLOCK = 64
EPS = 1e-05
SCORE_SCALE = HEAD_SIZE ** (-0.5) * math.log2(math.e)
PROJECT_VMEM = 8 * 1024 * 1024
ATTEND_VMEM = 20 * 1024 * 1024
WHOLE = pl.BlockSpec(memory_space=pltpu.VMEM)
IN_PLACE = pl.BlockSpec(memory_space=pl.ANY)
HEADS_OUT = 4


def turned(value, axis, by, wraps=True):
    length = lax.axis_size(axis)
    pairs = [(i, (i + by) % length) for i in range(length) if wraps or i + by < length]
    return lax.ppermute(value, axis, pairs)


def write_keys_values(keys, values, gain_ref, out_ref):
    width = keys.shape[1]
    for head in range(width // HEAD_SIZE):
        at = slice(head * HEAD_SIZE, (head + 1) * HEAD_SIZE)
        own = keys[:, at]
        mean = jnp.mean(own * own, axis=-1, keepdims=True)
        out_ref[:, at] = (own * lax.rsqrt(mean + EPS) * gain_ref[...]).astype(out_ref.dtype)
    out_ref[:, width:] = values.astype(out_ref.dtype)


def project_cost(rows, key_matrix):
    size = math.prod(key_matrix.shape)
    return pl.CostEstimate(flops=4 * rows * size, transcendentals=0, bytes_accessed=4 * size)


def project_kernel(*refs):
    *row_refs, key_ref, value_ref, gain_ref, out_ref = refs
    rows = [ref[...] for ref in row_refs]
    rows = rows[0] if len(rows) == 1 else jnp.concatenate(rows, axis=0)
    keys = jnp.dot(rows, key_ref[...], preferred_element_type=jnp.float32)
    values = jnp.dot(rows, value_ref[...], preferred_element_type=jnp.float32)
    write_keys_values(keys, values, gain_ref, out_ref)


def project(row_parts, key_matrix, value_matrix, key_gain, name):
    width = key_matrix.shape[1]
    rows = sum(each.shape[0] for each in row_parts)
    return pl.pallas_call(
        project_kernel,
        out_shape=jax.ShapeDtypeStruct((rows, 2 * width), jnp.bfloat16),
        in_specs=[WHOLE] * (len(row_parts) + 3),
        out_specs=WHOLE,
        cost_estimate=project_cost(rows, key_matrix),
        compiler_params=pltpu.CompilerParams(vmem_limit_bytes=PROJECT_VMEM),
        name=name,
    )(*row_parts, key_matrix, value_matrix, key_gain)


def last_half_kernel(rows_ref, key_ref, value_ref, out_ref):
    depth, width = rows_ref.shape[1], key_ref.shape[1]
    rows = rows_ref[...]
    out_ref[:, :width] = jnp.dot(rows, key_ref[depth:], preferred_element_type=jnp.float32)
    out_ref[:, width:] = jnp.dot(rows, value_ref[depth:], preferred_element_type=jnp.float32)


def first_half_kernel(rows_ref, sums_ref, key_ref, value_ref, gain_ref, out_ref):
    depth, width = rows_ref.shape[1], key_ref.shape[1]
    rows = rows_ref[...]
    keys = jnp.dot(rows, key_ref[:depth], preferred_element_type=jnp.float32)
    values = jnp.dot(rows, value_ref[:depth], preferred_element_type=jnp.float32)
    write_keys_values(
        sums_ref[:, :width] + keys, sums_ref[:, width:] + values, gain_ref, out_ref
    )


def project_by_halves(first_half, last_half, key_matrix, value_matrix, key_gain, name):
    rows, width = first_half.shape[0], key_matrix.shape[1]
    params = dict(
        out_specs=WHOLE,
        cost_estimate=project_cost(rows // 2, key_matrix),
        compiler_params=pltpu.CompilerParams(vmem_limit_bytes=PROJECT_VMEM),
    )
    sums = pl.pallas_call(
        last_half_kernel,
        out_shape=jax.ShapeDtypeStruct((rows, 2 * width), jnp.float32),
        in_specs=[WHOLE] * 3,
        name=name + "_last_half",
        **params,
    )(last_half, key_matrix, value_matrix)
    first_half = after(first_half, sums)
    return pl.pallas_call(
        first_half_kernel,
        out_shape=jax.ShapeDtypeStruct((rows, 2 * width), jnp.bfloat16),
        in_specs=[WHOLE] * 5,
        name=name + "_first_half",
        **params,
    )(first_half, sums, key_matrix, value_matrix, key_gain)


def attend_kernel(first, last, kv_heads, *refs):
    refs = list(refs)
    copies = []
    if last:
        sems, held = refs.pop(), refs.pop()
    query_ref = refs.pop(0)
    block_refs = [refs.pop(0) for _ in range(REACH)]
    open_ref = refs.pop(0)
    if first:
        gain_ref, normed_ref = refs.pop(0), refs.pop(0)
    else:
        sums_in, totals_in = refs.pop(0), refs.pop(0)
    rows = query_ref.shape[0]
    count = block_refs[0].shape[0]
    group = query_ref.shape[1] // HEAD_SIZE // kv_heads
    image = lax.broadcasted_iota(jnp.int32, (rows, REACH * count), 1) // count
    is_open = jnp.zeros((rows, REACH * count), jnp.float32)
    for at in range(REACH):
        is_open = jnp.where(image == at, open_ref[:, at : at + 1], is_open)
    is_open = jnp.concatenate([is_open] * group, axis=0)
    lane = lax.broadcasted_iota(jnp.int32, (rows, HEAD_SIZE), 1)
    totals = jnp.zeros((rows, HEAD_SIZE), jnp.float32)

    def columns(head):
        return slice(head * HEAD_SIZE, (head + 1) * HEAD_SIZE)

    for kv_head in range(kv_heads):
        heads = range(kv_head * group, (kv_head + 1) * group)
        keys = jnp.concatenate([ref[:, columns(kv_head)] for ref in block_refs], axis=0)
        values = jnp.concatenate(
            [ref[:, columns(kv_heads + kv_head)] for ref in block_refs], axis=0
        )
        values = jnp.concatenate([values, jnp.ones_like(values)], axis=1)
        queries = []
        for head in heads:
            query = query_ref[:, columns(head)]
            if first:
                raw = query.astype(jnp.float32)
                mean = jnp.mean(raw * raw, axis=-1, keepdims=True)
                query = (raw * lax.rsqrt(mean + EPS) * gain_ref[...]).astype(jnp.bfloat16)
                normed_ref[:, columns(head)] = query
            queries.append(query)
        scores = lax.dot_general(
            jnp.concatenate(queries, axis=0),
            keys,
            (((1,), (1,)), ((), ())),
            preferred_element_type=jnp.float32,
        )
        weights = (jnp.exp2(scores) * is_open).astype(jnp.bfloat16)
        both = jnp.dot(weights, values, preferred_element_type=jnp.float32)
        for at, head in enumerate(heads):
            sums = both[at * rows : (at + 1) * rows, :HEAD_SIZE]
            total = both[at * rows : (at + 1) * rows, HEAD_SIZE:]
            if not first:
                sums = sums + sums_in[:, columns(head)]
                total = total + totals_in[:, head : head + 1]
            if last:
                safe = jnp.where(total > 0, total, jnp.ones_like(total))
                inverse = pl.reciprocal(safe, approx=True)
                inverse = inverse * (2.0 - safe * inverse)
                held[:, columns(head)] = (sums * inverse).astype(jnp.bfloat16)
                if head % HEADS_OUT == HEADS_OUT - 1:
                    part = pl.ds((head + 1 - HEADS_OUT) * HEAD_SIZE, HEADS_OUT * HEAD_SIZE)
                    copies.append(
                        pltpu.make_async_copy(
                            held.at[:, part], refs[0].at[:, part], sems.at[head // HEADS_OUT]
                        )
                    )
                    copies[-1].start()
            else:
                refs[0][:, columns(head)] = sums
                totals = jnp.where(lane == head, total, totals)
    if not last:
        refs[1][...] = totals
    for copy in copies:
        copy.wait()


def attend_cost(rows, width, keys):
    return pl.CostEstimate(
        flops=16 * rows * width * keys,
        transcendentals=rows * width // HEAD_SIZE * keys,
        bytes_accessed=2 * rows * width,
    )


def attend(query, blocks, is_open, gain, carried, last, name):
    first = carried is None
    rows, width = query.shape
    kv_heads = blocks[0].shape[1] // (2 * HEAD_SIZE)
    operands = [query, *blocks, is_open] + ([gain] if first else list(carried))
    scratch_shapes = []
    if last:
        out_shape = [jax.ShapeDtypeStruct((rows, width), jnp.bfloat16)]
        scratch_shapes.append(pltpu.VMEM((rows, width), jnp.bfloat16))
        scratch_shapes.append(pltpu.SemaphoreType.DMA((width // (HEADS_OUT * HEAD_SIZE),)))
    else:
        out_shape = [
            jax.ShapeDtypeStruct((rows, width), jnp.float32),
            jax.ShapeDtypeStruct((rows, HEAD_SIZE), jnp.float32),
        ]
    if first:
        out_shape.insert(0, jax.ShapeDtypeStruct((rows, width), jnp.bfloat16))
    return pl.pallas_call(
        functools.partial(attend_kernel, first, last, kv_heads),
        out_shape=out_shape,
        in_specs=[WHOLE] * len(operands),
        out_specs=[IN_PLACE if last else WHOLE] * len(out_shape),
        scratch_shapes=scratch_shapes,
        cost_estimate=attend_cost(rows, width, REACH * blocks[0].shape[0]),
        compiler_params=pltpu.CompilerParams(vmem_limit_bytes=ATTEND_VMEM),
        name=name,
    )(*operands)


def after(values, *others):
    return lax.optimization_barrier((values, others))[0]


def body(
    text_query_matrix, vision, key_matrix, value_matrix, query_norm_gain, key_gain, block_mask
):
    position = lax.axis_index("seq")
    images = lax.broadcasted_iota(jnp.int32, (1, block_mask.shape[1], REACH), 1)
    wanted = position - lax.broadcasted_iota(jnp.int32, (1, block_mask.shape[1], REACH), 2)
    is_open = jnp.sum(jnp.where(images == wanted, block_mask[:, :, None], 0), axis=1)
    is_open = jnp.repeat(is_open.astype(jnp.float32), BLOCK, axis=0)
    query_gain = (query_norm_gain * SCORE_SCALE).reshape(1, HEAD_SIZE)
    key_gain = key_gain.reshape(1, HEAD_SIZE)

    def projected(row_parts, name):
        return project(row_parts, key_matrix, value_matrix, key_gain, "project_" + name)

    def reached(block, wraps=True):
        return [block] + [turned(block, "seq", by, wraps) for by in range(1, REACH)]

    left = turned(vision, "tp", 1)
    right = turned(vision, "tp", -1)
    own = projected([vision], "own")
    own_blocks = reached(own, wraps=False)
    normed, *carried = attend(
        text_query_matrix, own_blocks, is_open, query_gain, None, False, "attend_own"
    )

    half = vision.shape[1] // 2
    right = after(right, carried)
    last_half = turned(right[:, half:], "tp", -1)
    left = after(left, carried)
    first_half = turned(left[:, :half], "tp", 1)
    sides = projected([left, right], "sides")
    side_blocks = reached(sides)
    last_half = after(last_half, sides)
    across = project_by_halves(
        first_half, last_half, key_matrix, value_matrix, key_gain, "project_across"
    )
    across_blocks = reached(across)
    side_blocks = after(side_blocks, across)
    carried = attend(normed, side_blocks, is_open, None, carried, False, "attend_sides")
    across_blocks = after(across_blocks, carried)
    (result,) = attend(normed, across_blocks, is_open, None, carried, True, "attend_across")
    return result


def solution(mesh):
    placed = (
        P("seq", "tp"),
        P(("seq", "tp"), None),
        P(None, "tp"),
        P(None, "tp"),
        P(),
        P(),
        P("seq", None),
    )
    return jax.shard_map(
        body, mesh=mesh, in_specs=placed, out_specs=P("seq", "tp"), check_vma=False
    )
```

```python
import functools
import math

import jax
import jax.numpy as jnp
from jax import lax
from jax.experimental import pallas as pl
from jax.experimental.pallas import tpu as pltpu
from jax.sharding import PartitionSpec as P

HEAD_SIZE = 128
REACH = 4
BLOCK = 64
EPS = 1e-05
SCORE_SCALE = HEAD_SIZE ** (-0.5) * math.log2(math.e)
PROJECT_VMEM = 8 * 1024 * 1024
ATTEND_VMEM = 20 * 1024 * 1024
WHOLE = pl.BlockSpec(memory_space=pltpu.VMEM)
IN_PLACE = pl.BlockSpec(memory_space=pl.ANY)
HEADS_OUT = 4


def turned(value, axis, by, wraps=True):
    length = lax.axis_size(axis)
    pairs = [(i, (i + by) % length) for i in range(length) if wraps or i + by < length]
    return lax.ppermute(value, axis, pairs)


def write_keys_values(keys, values, gain_ref, out_ref):
    width = keys.shape[1]
    for head in range(width // HEAD_SIZE):
        at = slice(head * HEAD_SIZE, (head + 1) * HEAD_SIZE)
        own = keys[:, at]
        mean = jnp.mean(own * own, axis=-1, keepdims=True)
        out_ref[:, at] = (own * lax.rsqrt(mean + EPS) * gain_ref[...]).astype(out_ref.dtype)
    out_ref[:, width:] = values.astype(out_ref.dtype)


def project_cost(rows, key_matrix):
    size = math.prod(key_matrix.shape)
    return pl.CostEstimate(flops=4 * rows * size, transcendentals=0, bytes_accessed=4 * size)


def project_kernel(*refs):
    *row_refs, key_ref, value_ref, gain_ref, out_ref = refs
    rows = [ref[...] for ref in row_refs]
    rows = rows[0] if len(rows) == 1 else jnp.concatenate(rows, axis=0)
    keys = jnp.dot(rows, key_ref[...], preferred_element_type=jnp.float32)
    values = jnp.dot(rows, value_ref[...], preferred_element_type=jnp.float32)
    write_keys_values(keys, values, gain_ref, out_ref)


def project(row_parts, key_matrix, value_matrix, key_gain, name):
    width = key_matrix.shape[1]
    rows = sum(each.shape[0] for each in row_parts)
    return pl.pallas_call(
        project_kernel,
        out_shape=jax.ShapeDtypeStruct((rows, 2 * width), jnp.bfloat16),
        in_specs=[WHOLE] * (len(row_parts) + 3),
        out_specs=WHOLE,
        cost_estimate=project_cost(rows, key_matrix),
        compiler_params=pltpu.CompilerParams(vmem_limit_bytes=PROJECT_VMEM),
        name=name,
    )(*row_parts, key_matrix, value_matrix, key_gain)


def last_half_kernel(rows_ref, key_ref, value_ref, out_ref):
    depth, width = rows_ref.shape[1], key_ref.shape[1]
    rows = rows_ref[...]
    out_ref[:, :width] = jnp.dot(rows, key_ref[depth:], preferred_element_type=jnp.float32)
    out_ref[:, width:] = jnp.dot(rows, value_ref[depth:], preferred_element_type=jnp.float32)


def first_half_kernel(rows_ref, sums_ref, key_ref, value_ref, gain_ref, out_ref):
    depth, width = rows_ref.shape[1], key_ref.shape[1]
    rows = rows_ref[...]
    keys = jnp.dot(rows, key_ref[:depth], preferred_element_type=jnp.float32)
    values = jnp.dot(rows, value_ref[:depth], preferred_element_type=jnp.float32)
    write_keys_values(
        sums_ref[:, :width] + keys, sums_ref[:, width:] + values, gain_ref, out_ref
    )


def project_by_halves(first_half, last_half, key_matrix, value_matrix, key_gain, name):
    rows, width = first_half.shape[0], key_matrix.shape[1]
    params = dict(
        out_specs=WHOLE,
        cost_estimate=project_cost(rows // 2, key_matrix),
        compiler_params=pltpu.CompilerParams(vmem_limit_bytes=PROJECT_VMEM),
    )
    sums = pl.pallas_call(
        last_half_kernel,
        out_shape=jax.ShapeDtypeStruct((rows, 2 * width), jnp.float32),
        in_specs=[WHOLE] * 3,
        name=name + "_last_half",
        **params,
    )(last_half, key_matrix, value_matrix)
    first_half = after(first_half, sums)
    return pl.pallas_call(
        first_half_kernel,
        out_shape=jax.ShapeDtypeStruct((rows, 2 * width), jnp.bfloat16),
        in_specs=[WHOLE] * 5,
        name=name + "_first_half",
        **params,
    )(first_half, sums, key_matrix, value_matrix, key_gain)


def attend_kernel(first, last, kv_heads, *refs):
    refs = list(refs)
    copies = []
    if last:
        sems, held = refs.pop(), refs.pop()
    query_ref = refs.pop(0)
    block_refs = [refs.pop(0) for _ in range(REACH)]
    open_ref = refs.pop(0)
    if first:
        gain_ref, normed_ref = refs.pop(0), refs.pop(0)
    else:
        sums_in, totals_in = refs.pop(0), refs.pop(0)
    rows = query_ref.shape[0]
    count = block_refs[0].shape[0]
    group = query_ref.shape[1] // HEAD_SIZE // kv_heads
    image = lax.broadcasted_iota(jnp.int32, (rows, REACH * count), 1) // count
    is_open = jnp.zeros((rows, REACH * count), jnp.float32)
    for at in range(REACH):
        is_open = jnp.where(image == at, open_ref[:, at : at + 1], is_open)
    is_open = jnp.concatenate([is_open] * group, axis=0)
    lane = lax.broadcasted_iota(jnp.int32, (rows, HEAD_SIZE), 1)
    totals = jnp.zeros((rows, HEAD_SIZE), jnp.float32)

    def columns(head):
        return slice(head * HEAD_SIZE, (head + 1) * HEAD_SIZE)

    for kv_head in range(kv_heads):
        heads = range(kv_head * group, (kv_head + 1) * group)
        keys = jnp.concatenate([ref[:, columns(kv_head)] for ref in block_refs], axis=0)
        values = jnp.concatenate(
            [ref[:, columns(kv_heads + kv_head)] for ref in block_refs], axis=0
        )
        values = jnp.concatenate([values, jnp.ones_like(values)], axis=1)
        queries = []
        for head in heads:
            query = query_ref[:, columns(head)]
            if first:
                raw = query.astype(jnp.float32)
                mean = jnp.mean(raw * raw, axis=-1, keepdims=True)
                query = (raw * lax.rsqrt(mean + EPS) * gain_ref[...]).astype(jnp.bfloat16)
                normed_ref[:, columns(head)] = query
            queries.append(query)
        scores = lax.dot_general(
            jnp.concatenate(queries, axis=0),
            keys,
            (((1,), (1,)), ((), ())),
            preferred_element_type=jnp.float32,
        )
        weights = (jnp.exp2(scores) * is_open).astype(jnp.bfloat16)
        both = jnp.dot(weights, values, preferred_element_type=jnp.float32)
        both = [both[at * rows : (at + 1) * rows] for at in range(group)]
        for at, head in enumerate(heads):
            totals = jnp.where(lane == head, both[at][:, HEAD_SIZE:], totals)
        if last:
            whole = totals + totals_in[...]
            safe = jnp.where(whole > 0, whole, jnp.ones_like(whole))
            inverse = pl.reciprocal(safe, approx=True)
            inverse = inverse * (2.0 - safe * inverse)
        for at, head in enumerate(heads):
            sums = both[at][:, :HEAD_SIZE]
            if not first:
                sums = sums + sums_in[:, columns(head)]
            if last:
                result = sums * inverse[:, head : head + 1]
                held[:, columns(head)] = result.astype(jnp.bfloat16)
                if head % HEADS_OUT == HEADS_OUT - 1:
                    part = pl.ds((head + 1 - HEADS_OUT) * HEAD_SIZE, HEADS_OUT * HEAD_SIZE)
                    copies.append(
                        pltpu.make_async_copy(
                            held.at[:, part], refs[0].at[:, part], sems.at[head // HEADS_OUT]
                        )
                    )
                    copies[-1].start()
            else:
                refs[0][:, columns(head)] = sums
    if not first:
        totals = totals + totals_in[...]
    if not last:
        refs[1][...] = totals
    for copy in copies:
        copy.wait()


def attend_cost(rows, width, keys):
    return pl.CostEstimate(
        flops=16 * rows * width * keys,
        transcendentals=rows * width // HEAD_SIZE * keys,
        bytes_accessed=2 * rows * width,
    )


def attend(query, blocks, is_open, gain, carried, last, name):
    first = carried is None
    rows, width = query.shape
    kv_heads = blocks[0].shape[1] // (2 * HEAD_SIZE)
    operands = [query, *blocks, is_open] + ([gain] if first else list(carried))
    scratch_shapes = []
    if last:
        out_shape = [jax.ShapeDtypeStruct((rows, width), jnp.bfloat16)]
        scratch_shapes.append(pltpu.VMEM((rows, width), jnp.bfloat16))
        scratch_shapes.append(pltpu.SemaphoreType.DMA((width // (HEADS_OUT * HEAD_SIZE),)))
    else:
        out_shape = [
            jax.ShapeDtypeStruct((rows, width), jnp.float32),
            jax.ShapeDtypeStruct((rows, HEAD_SIZE), jnp.float32),
        ]
    if first:
        out_shape.insert(0, jax.ShapeDtypeStruct((rows, width), jnp.bfloat16))
    return pl.pallas_call(
        functools.partial(attend_kernel, first, last, kv_heads),
        out_shape=out_shape,
        in_specs=[WHOLE] * len(operands),
        out_specs=[IN_PLACE if last else WHOLE] * len(out_shape),
        scratch_shapes=scratch_shapes,
        cost_estimate=attend_cost(rows, width, REACH * blocks[0].shape[0]),
        compiler_params=pltpu.CompilerParams(vmem_limit_bytes=ATTEND_VMEM),
        name=name,
    )(*operands)


def after(values, *others):
    return lax.optimization_barrier((values, others))[0]


def body(
    text_query_matrix, vision, key_matrix, value_matrix, query_norm_gain, key_gain, block_mask
):
    position = lax.axis_index("seq")
    images = lax.broadcasted_iota(jnp.int32, (1, block_mask.shape[1], REACH), 1)
    wanted = position - lax.broadcasted_iota(jnp.int32, (1, block_mask.shape[1], REACH), 2)
    is_open = jnp.sum(jnp.where(images == wanted, block_mask[:, :, None], 0), axis=1)
    is_open = jnp.repeat(is_open.astype(jnp.float32), BLOCK, axis=0)
    query_gain = (query_norm_gain * SCORE_SCALE).reshape(1, HEAD_SIZE)
    key_gain = key_gain.reshape(1, HEAD_SIZE)

    def projected(row_parts, name):
        return project(row_parts, key_matrix, value_matrix, key_gain, "project_" + name)

    def reached(block, wraps=True):
        return [block] + [turned(block, "seq", by, wraps) for by in range(1, REACH)]

    left = turned(vision, "tp", 1)
    right = turned(vision, "tp", -1)
    own = projected([vision], "own")
    own_blocks = reached(own, wraps=False)
    normed, *carried = attend(
        text_query_matrix, own_blocks, is_open, query_gain, None, False, "attend_own"
    )

    half = vision.shape[1] // 2
    right = after(right, carried)
    last_half = turned(right[:, half:], "tp", -1)
    left = after(left, carried)
    first_half = turned(left[:, :half], "tp", 1)
    sides = projected([left, right], "sides")
    side_blocks = reached(sides)
    last_half = after(last_half, sides)
    across = project_by_halves(
        first_half, last_half, key_matrix, value_matrix, key_gain, "project_across"
    )
    across_blocks = reached(across)
    side_blocks = after(side_blocks, across)
    carried = attend(normed, side_blocks, is_open, None, carried, False, "attend_sides")
    across_blocks = after(across_blocks, carried)
    (result,) = attend(normed, across_blocks, is_open, None, carried, True, "attend_across")
    return result


def solution(mesh):
    placed = (
        P("seq", "tp"),
        P(("seq", "tp"), None),
        P(None, "tp"),
        P(None, "tp"),
        P(),
        P(),
        P("seq", None),
    )
    return jax.shard_map(
        body, mesh=mesh, in_specs=placed, out_specs=P("seq", "tp"), check_vma=False
    )
```

```python
import functools
import math

import jax
import jax.numpy as jnp
from jax import lax
from jax.experimental import pallas as pl
from jax.experimental.pallas import tpu as pltpu
from jax.sharding import PartitionSpec as P

HEAD_SIZE = 128
REACH = 4
BLOCK = 64
EPS = 1e-05
SCORE_SCALE = HEAD_SIZE ** (-0.5) * math.log2(math.e)
PROJECT_VMEM = 8 * 1024 * 1024
ATTEND_VMEM = 20 * 1024 * 1024
WHOLE = pl.BlockSpec(memory_space=pltpu.VMEM)
IN_PLACE = pl.BlockSpec(memory_space=pl.ANY)
HEADS_OUT = 4


def turned(value, axis, by, wraps=True):
    length = lax.axis_size(axis)
    pairs = [(i, (i + by) % length) for i in range(length) if wraps or i + by < length]
    return lax.ppermute(value, axis, pairs)


def sent(value, axis, target):
    length = lax.axis_size(axis)
    return lax.ppermute(value, axis, [(i, target(i) % length) for i in range(length)])


def paired_by_core(block):
    two_chips = sent(block, "seq", lambda s: s + 1 + 2 * (s % 2))
    other_core = sent(block, "seq", lambda s: s + 3 - 2 * (s % 2))
    same_core = turned(block, "seq", 2)
    return [block, same_core, other_core, two_chips]


def paired_distances(position, at):
    two_chips = jnp.where(position % 2 == 0, 3, 1)
    return jnp.where(at == 3, two_chips, jnp.where(at == 2, 4 - two_chips, jnp.where(at == 1, 2, 0)))


def open_columns(block_mask, position, distances):
    images = lax.broadcasted_iota(jnp.int32, (1, block_mask.shape[1], REACH), 1)
    at = lax.broadcasted_iota(jnp.int32, (1, block_mask.shape[1], REACH), 2)
    wanted = position - distances(position, at)
    is_open = jnp.sum(jnp.where(images == wanted, block_mask[:, :, None], 0), axis=1)
    return jnp.repeat(is_open.astype(jnp.float32), BLOCK, axis=0)


def write_keys_values(keys, values, gain_ref, out_ref):
    width = keys.shape[1]
    for head in range(width // HEAD_SIZE):
        at = slice(head * HEAD_SIZE, (head + 1) * HEAD_SIZE)
        own = keys[:, at]
        mean = jnp.mean(own * own, axis=-1, keepdims=True)
        out_ref[:, at] = (own * lax.rsqrt(mean + EPS) * gain_ref[...]).astype(out_ref.dtype)
    out_ref[:, width:] = values.astype(out_ref.dtype)


def project_cost(rows, key_matrix):
    size = math.prod(key_matrix.shape)
    return pl.CostEstimate(flops=4 * rows * size, transcendentals=0, bytes_accessed=4 * size)


def project_kernel(*refs):
    *row_refs, key_ref, value_ref, gain_ref, out_ref = refs
    rows = [ref[...] for ref in row_refs]
    rows = rows[0] if len(rows) == 1 else jnp.concatenate(rows, axis=0)
    keys = jnp.dot(rows, key_ref[...], preferred_element_type=jnp.float32)
    values = jnp.dot(rows, value_ref[...], preferred_element_type=jnp.float32)
    write_keys_values(keys, values, gain_ref, out_ref)


def project(row_parts, key_matrix, value_matrix, key_gain, name):
    width = key_matrix.shape[1]
    rows = sum(each.shape[0] for each in row_parts)
    return pl.pallas_call(
        project_kernel,
        out_shape=jax.ShapeDtypeStruct((rows, 2 * width), jnp.bfloat16),
        in_specs=[WHOLE] * (len(row_parts) + 3),
        out_specs=WHOLE,
        cost_estimate=project_cost(rows, key_matrix),
        compiler_params=pltpu.CompilerParams(vmem_limit_bytes=PROJECT_VMEM),
        name=name,
    )(*row_parts, key_matrix, value_matrix, key_gain)


def last_half_kernel(rows_ref, key_ref, value_ref, out_ref):
    depth, width = rows_ref.shape[1], key_ref.shape[1]
    rows = rows_ref[...]
    out_ref[:, :width] = jnp.dot(rows, key_ref[depth:], preferred_element_type=jnp.float32)
    out_ref[:, width:] = jnp.dot(rows, value_ref[depth:], preferred_element_type=jnp.float32)


def first_half_kernel(rows_ref, sums_ref, key_ref, value_ref, gain_ref, out_ref):
    depth, width = rows_ref.shape[1], key_ref.shape[1]
    rows = rows_ref[...]
    keys = jnp.dot(rows, key_ref[:depth], preferred_element_type=jnp.float32)
    values = jnp.dot(rows, value_ref[:depth], preferred_element_type=jnp.float32)
    write_keys_values(
        sums_ref[:, :width] + keys, sums_ref[:, width:] + values, gain_ref, out_ref
    )


def project_by_halves(first_half, last_half, key_matrix, value_matrix, key_gain, name):
    rows, width = first_half.shape[0], key_matrix.shape[1]
    params = dict(
        out_specs=WHOLE,
        cost_estimate=project_cost(rows // 2, key_matrix),
        compiler_params=pltpu.CompilerParams(vmem_limit_bytes=PROJECT_VMEM),
    )
    sums = pl.pallas_call(
        last_half_kernel,
        out_shape=jax.ShapeDtypeStruct((rows, 2 * width), jnp.float32),
        in_specs=[WHOLE] * 3,
        name=name + "_last_half",
        **params,
    )(last_half, key_matrix, value_matrix)
    first_half = after(first_half, sums)
    return pl.pallas_call(
        first_half_kernel,
        out_shape=jax.ShapeDtypeStruct((rows, 2 * width), jnp.bfloat16),
        in_specs=[WHOLE] * 5,
        name=name + "_first_half",
        **params,
    )(first_half, sums, key_matrix, value_matrix, key_gain)


def attend_kernel(first, last, kv_heads, *refs):
    refs = list(refs)
    copies = []
    if last:
        sems, held = refs.pop(), refs.pop()
    query_ref = refs.pop(0)
    block_refs = [refs.pop(0) for _ in range(REACH)]
    open_ref = refs.pop(0)
    if first:
        gain_ref, normed_ref = refs.pop(0), refs.pop(0)
    else:
        sums_in, totals_in = refs.pop(0), refs.pop(0)
    rows = query_ref.shape[0]
    count = block_refs[0].shape[0]
    group = query_ref.shape[1] // HEAD_SIZE // kv_heads
    image = lax.broadcasted_iota(jnp.int32, (rows, REACH * count), 1) // count
    is_open = jnp.zeros((rows, REACH * count), jnp.float32)
    for at in range(REACH):
        is_open = jnp.where(image == at, open_ref[:, at : at + 1], is_open)
    is_open = jnp.concatenate([is_open] * group, axis=0)
    lane = lax.broadcasted_iota(jnp.int32, (rows, HEAD_SIZE), 1)
    totals = jnp.zeros((rows, HEAD_SIZE), jnp.float32)

    def columns(head):
        return slice(head * HEAD_SIZE, (head + 1) * HEAD_SIZE)

    for kv_head in range(kv_heads):
        heads = range(kv_head * group, (kv_head + 1) * group)
        keys = jnp.concatenate([ref[:, columns(kv_head)] for ref in block_refs], axis=0)
        values = jnp.concatenate(
            [ref[:, columns(kv_heads + kv_head)] for ref in block_refs], axis=0
        )
        values = jnp.concatenate([values, jnp.ones_like(values)], axis=1)
        queries = []
        for head in heads:
            query = query_ref[:, columns(head)]
            if first:
                raw = query.astype(jnp.float32)
                mean = jnp.mean(raw * raw, axis=-1, keepdims=True)
                query = (raw * lax.rsqrt(mean + EPS) * gain_ref[...]).astype(jnp.bfloat16)
                normed_ref[:, columns(head)] = query
            queries.append(query)
        scores = lax.dot_general(
            jnp.concatenate(queries, axis=0),
            keys,
            (((1,), (1,)), ((), ())),
            preferred_element_type=jnp.float32,
        )
        weights = (jnp.exp2(scores) * is_open).astype(jnp.bfloat16)
        both = jnp.dot(weights, values, preferred_element_type=jnp.float32)
        for at, head in enumerate(heads):
            sums = both[at * rows : (at + 1) * rows, :HEAD_SIZE]
            total = both[at * rows : (at + 1) * rows, HEAD_SIZE:]
            if not first:
                sums = sums + sums_in[:, columns(head)]
                total = total + totals_in[:, head : head + 1]
            if last:
                safe = jnp.where(total > 0, total, jnp.ones_like(total))
                inverse = pl.reciprocal(safe, approx=True)
                inverse = inverse * (2.0 - safe * inverse)
                held[:, columns(head)] = (sums * inverse).astype(jnp.bfloat16)
                if head % HEADS_OUT == HEADS_OUT - 1:
                    part = pl.ds((head + 1 - HEADS_OUT) * HEAD_SIZE, HEADS_OUT * HEAD_SIZE)
                    copies.append(
                        pltpu.make_async_copy(
                            held.at[:, part], refs[0].at[:, part], sems.at[head // HEADS_OUT]
                        )
                    )
                    copies[-1].start()
            else:
                refs[0][:, columns(head)] = sums
                totals = jnp.where(lane == head, total, totals)
    if not last:
        refs[1][...] = totals
    for copy in copies:
        copy.wait()


def attend_cost(rows, width, keys):
    return pl.CostEstimate(
        flops=16 * rows * width * keys,
        transcendentals=rows * width // HEAD_SIZE * keys,
        bytes_accessed=2 * rows * width,
    )


def attend(query, blocks, is_open, gain, carried, last, name):
    first = carried is None
    rows, width = query.shape
    kv_heads = blocks[0].shape[1] // (2 * HEAD_SIZE)
    operands = [query, *blocks, is_open] + ([gain] if first else list(carried))
    scratch_shapes = []
    if last:
        out_shape = [jax.ShapeDtypeStruct((rows, width), jnp.bfloat16)]
        scratch_shapes.append(pltpu.VMEM((rows, width), jnp.bfloat16))
        scratch_shapes.append(pltpu.SemaphoreType.DMA((width // (HEADS_OUT * HEAD_SIZE),)))
    else:
        out_shape = [
            jax.ShapeDtypeStruct((rows, width), jnp.float32),
            jax.ShapeDtypeStruct((rows, HEAD_SIZE), jnp.float32),
        ]
    if first:
        out_shape.insert(0, jax.ShapeDtypeStruct((rows, width), jnp.bfloat16))
    return pl.pallas_call(
        functools.partial(attend_kernel, first, last, kv_heads),
        out_shape=out_shape,
        in_specs=[WHOLE] * len(operands),
        out_specs=[IN_PLACE if last else WHOLE] * len(out_shape),
        scratch_shapes=scratch_shapes,
        cost_estimate=attend_cost(rows, width, REACH * blocks[0].shape[0]),
        compiler_params=pltpu.CompilerParams(vmem_limit_bytes=ATTEND_VMEM),
        name=name,
    )(*operands)


def after(values, *others):
    return lax.optimization_barrier((values, others))[0]


def body(
    text_query_matrix, vision, key_matrix, value_matrix, query_norm_gain, key_gain, block_mask
):
    position = lax.axis_index("seq")
    is_open = open_columns(block_mask, position, lambda position, at: at)
    query_gain = (query_norm_gain * SCORE_SCALE).reshape(1, HEAD_SIZE)
    key_gain = key_gain.reshape(1, HEAD_SIZE)

    def projected(row_parts, name):
        return project(row_parts, key_matrix, value_matrix, key_gain, "project_" + name)

    def reached(block, wraps=True):
        return [block] + [turned(block, "seq", by, wraps) for by in range(1, REACH)]

    left = turned(vision, "tp", 1)
    right = turned(vision, "tp", -1)
    own = projected([vision], "own")
    own_blocks = reached(own, wraps=False)
    normed, *carried = attend(
        text_query_matrix, own_blocks, is_open, query_gain, None, False, "attend_own"
    )

    half = vision.shape[1] // 2
    right = after(right, carried)
    last_half = turned(right[:, half:], "tp", -1)
    left = after(left, carried)
    first_half = turned(left[:, :half], "tp", 1)
    sides = projected([left, right], "sides")
    side_blocks = reached(sides)
    last_half = after(last_half, sides)
    across = project_by_halves(
        first_half, last_half, key_matrix, value_matrix, key_gain, "project_across"
    )
    across_blocks = paired_by_core(across)
    is_open_paired = open_columns(after(block_mask, sides), position, paired_distances)
    side_blocks = after(side_blocks, across)
    carried = attend(normed, side_blocks, is_open, None, carried, False, "attend_sides")
    across_blocks = after(across_blocks, carried)
    (result,) = attend(normed, across_blocks, is_open_paired, None, carried, True, "attend_across")
    return result


def solution(mesh):
    placed = (
        P("seq", "tp"),
        P(("seq", "tp"), None),
        P(None, "tp"),
        P(None, "tp"),
        P(),
        P(),
        P("seq", None),
    )
    return jax.shard_map(
        body, mesh=mesh, in_specs=placed, out_specs=P("seq", "tp"), check_vma=False
    )
```

```python
import functools
import math

import jax
import jax.numpy as jnp
from jax import lax
from jax.experimental import pallas as pl
from jax.experimental.pallas import tpu as pltpu
from jax.sharding import PartitionSpec as P

HEAD_SIZE = 128
REACH = 4
BLOCK = 64
EPS = 1e-05
SCORE_SCALE = HEAD_SIZE ** (-0.5) * math.log2(math.e)
PROJECT_VMEM = 8 * 1024 * 1024
ATTEND_VMEM = 20 * 1024 * 1024
WHOLE = pl.BlockSpec(memory_space=pltpu.VMEM)
IN_PLACE = pl.BlockSpec(memory_space=pl.ANY)
HEADS_OUT = 4


def turned(value, axis, by, wraps=True):
    length = lax.axis_size(axis)
    pairs = [(i, (i + by) % length) for i in range(length) if wraps or i + by < length]
    return lax.ppermute(value, axis, pairs)


def write_keys_values(keys, values, gain_ref, out_ref):
    width = keys.shape[1]
    for head in range(width // HEAD_SIZE):
        at = slice(head * HEAD_SIZE, (head + 1) * HEAD_SIZE)
        own = keys[:, at]
        mean = jnp.mean(own * own, axis=-1, keepdims=True)
        out_ref[:, at] = (own * lax.rsqrt(mean + EPS) * gain_ref[...]).astype(out_ref.dtype)
    out_ref[:, width:] = values.astype(out_ref.dtype)


def project_cost(rows, key_matrix):
    size = math.prod(key_matrix.shape)
    return pl.CostEstimate(flops=4 * rows * size, transcendentals=0, bytes_accessed=4 * size)


def project_kernel(*refs):
    *row_refs, key_ref, value_ref, gain_ref, out_ref = refs
    rows = [ref[...] for ref in row_refs]
    rows = rows[0] if len(rows) == 1 else jnp.concatenate(rows, axis=0)
    keys = jnp.dot(rows, key_ref[...], preferred_element_type=jnp.float32)
    values = jnp.dot(rows, value_ref[...], preferred_element_type=jnp.float32)
    write_keys_values(keys, values, gain_ref, out_ref)


def project(row_parts, key_matrix, value_matrix, key_gain, name):
    width = key_matrix.shape[1]
    rows = sum(each.shape[0] for each in row_parts)
    return pl.pallas_call(
        project_kernel,
        out_shape=jax.ShapeDtypeStruct((rows, 2 * width), jnp.bfloat16),
        in_specs=[WHOLE] * (len(row_parts) + 3),
        out_specs=WHOLE,
        cost_estimate=project_cost(rows, key_matrix),
        compiler_params=pltpu.CompilerParams(vmem_limit_bytes=PROJECT_VMEM),
        name=name,
    )(*row_parts, key_matrix, value_matrix, key_gain)


def last_half_kernel(rows_ref, key_ref, value_ref, out_ref):
    before, width = key_ref.shape[0] - rows_ref.shape[1], key_ref.shape[1]
    rows = rows_ref[...]
    out_ref[:, :width] = jnp.dot(rows, key_ref[before:], preferred_element_type=jnp.float32)
    out_ref[:, width:] = jnp.dot(rows, value_ref[before:], preferred_element_type=jnp.float32)


def first_half_kernel(rows_ref, sums_ref, key_ref, value_ref, gain_ref, out_ref):
    depth, width = rows_ref.shape[1], key_ref.shape[1]
    rows = rows_ref[...]
    keys = jnp.dot(rows, key_ref[:depth], preferred_element_type=jnp.float32)
    values = jnp.dot(rows, value_ref[:depth], preferred_element_type=jnp.float32)
    write_keys_values(
        sums_ref[:, :width] + keys, sums_ref[:, width:] + values, gain_ref, out_ref
    )


def project_by_halves(first_half, last_half, key_matrix, value_matrix, key_gain, name):
    rows, width = first_half.shape[0], key_matrix.shape[1]
    params = dict(
        out_specs=WHOLE,
        cost_estimate=project_cost(rows // 2, key_matrix),
        compiler_params=pltpu.CompilerParams(vmem_limit_bytes=PROJECT_VMEM),
    )
    sums = pl.pallas_call(
        last_half_kernel,
        out_shape=jax.ShapeDtypeStruct((rows, 2 * width), jnp.float32),
        in_specs=[WHOLE] * 3,
        name=name + "_last_half",
        **params,
    )(last_half, key_matrix, value_matrix)
    first_half = after(first_half, sums)
    return pl.pallas_call(
        first_half_kernel,
        out_shape=jax.ShapeDtypeStruct((rows, 2 * width), jnp.bfloat16),
        in_specs=[WHOLE] * 5,
        name=name + "_first_half",
        **params,
    )(first_half, sums, key_matrix, value_matrix, key_gain)


def attend_kernel(first, last, kv_heads, *refs):
    refs = list(refs)
    copies = []
    if last:
        sems, held = refs.pop(), refs.pop()
    query_ref = refs.pop(0)
    block_refs = [refs.pop(0) for _ in range(REACH)]
    open_ref = refs.pop(0)
    if first:
        gain_ref, normed_ref = refs.pop(0), refs.pop(0)
    else:
        sums_in, totals_in = refs.pop(0), refs.pop(0)
    rows = query_ref.shape[0]
    count = block_refs[0].shape[0]
    group = query_ref.shape[1] // HEAD_SIZE // kv_heads
    image = lax.broadcasted_iota(jnp.int32, (rows, REACH * count), 1) // count
    is_open = jnp.zeros((rows, REACH * count), jnp.float32)
    for at in range(REACH):
        is_open = jnp.where(image == at, open_ref[:, at : at + 1], is_open)
    is_open = jnp.concatenate([is_open] * group, axis=0)
    lane = lax.broadcasted_iota(jnp.int32, (rows, HEAD_SIZE), 1)
    totals = jnp.zeros((rows, HEAD_SIZE), jnp.float32)

    def columns(head):
        return slice(head * HEAD_SIZE, (head + 1) * HEAD_SIZE)

    for kv_head in range(kv_heads):
        heads = range(kv_head * group, (kv_head + 1) * group)
        keys = jnp.concatenate([ref[:, columns(kv_head)] for ref in block_refs], axis=0)
        values = jnp.concatenate(
            [ref[:, columns(kv_heads + kv_head)] for ref in block_refs], axis=0
        )
        values = jnp.concatenate([values, jnp.ones_like(values)], axis=1)
        queries = []
        for head in heads:
            query = query_ref[:, columns(head)]
            if first:
                raw = query.astype(jnp.float32)
                mean = jnp.mean(raw * raw, axis=-1, keepdims=True)
                query = (raw * lax.rsqrt(mean + EPS) * gain_ref[...]).astype(jnp.bfloat16)
                normed_ref[:, columns(head)] = query
            queries.append(query)
        scores = lax.dot_general(
            jnp.concatenate(queries, axis=0),
            keys,
            (((1,), (1,)), ((), ())),
            preferred_element_type=jnp.float32,
        )
        weights = (jnp.exp2(scores) * is_open).astype(jnp.bfloat16)
        both = jnp.dot(weights, values, preferred_element_type=jnp.float32)
        for at, head in enumerate(heads):
            sums = both[at * rows : (at + 1) * rows, :HEAD_SIZE]
            total = both[at * rows : (at + 1) * rows, HEAD_SIZE:]
            if not first:
                sums = sums + sums_in[:, columns(head)]
                total = total + totals_in[:, head : head + 1]
            if last:
                safe = jnp.where(total > 0, total, jnp.ones_like(total))
                inverse = pl.reciprocal(safe, approx=True)
                inverse = inverse * (2.0 - safe * inverse)
                held[:, columns(head)] = (sums * inverse).astype(jnp.bfloat16)
                if head % HEADS_OUT == HEADS_OUT - 1:
                    part = pl.ds((head + 1 - HEADS_OUT) * HEAD_SIZE, HEADS_OUT * HEAD_SIZE)
                    copies.append(
                        pltpu.make_async_copy(
                            held.at[:, part], refs[0].at[:, part], sems.at[head // HEADS_OUT]
                        )
                    )
                    copies[-1].start()
            else:
                refs[0][:, columns(head)] = sums
                totals = jnp.where(lane == head, total, totals)
    if not last:
        refs[1][...] = totals
    for copy in copies:
        copy.wait()


def attend_cost(rows, width, keys):
    return pl.CostEstimate(
        flops=16 * rows * width * keys,
        transcendentals=rows * width // HEAD_SIZE * keys,
        bytes_accessed=2 * rows * width,
    )


def attend(query, blocks, is_open, gain, carried, last, name):
    first = carried is None
    rows, width = query.shape
    kv_heads = blocks[0].shape[1] // (2 * HEAD_SIZE)
    operands = [query, *blocks, is_open] + ([gain] if first else list(carried))
    scratch_shapes = []
    if last:
        out_shape = [jax.ShapeDtypeStruct((rows, width), jnp.bfloat16)]
        scratch_shapes.append(pltpu.VMEM((rows, width), jnp.bfloat16))
        scratch_shapes.append(pltpu.SemaphoreType.DMA((width // (HEADS_OUT * HEAD_SIZE),)))
    else:
        out_shape = [
            jax.ShapeDtypeStruct((rows, width), jnp.float32),
            jax.ShapeDtypeStruct((rows, HEAD_SIZE), jnp.float32),
        ]
    if first:
        out_shape.insert(0, jax.ShapeDtypeStruct((rows, width), jnp.bfloat16))
    return pl.pallas_call(
        functools.partial(attend_kernel, first, last, kv_heads),
        out_shape=out_shape,
        in_specs=[WHOLE] * len(operands),
        out_specs=[IN_PLACE if last else WHOLE] * len(out_shape),
        scratch_shapes=scratch_shapes,
        cost_estimate=attend_cost(rows, width, REACH * blocks[0].shape[0]),
        compiler_params=pltpu.CompilerParams(vmem_limit_bytes=ATTEND_VMEM),
        name=name,
    )(*operands)


def after(values, *others):
    return lax.optimization_barrier((values, others))[0]


def body(
    text_query_matrix, vision, key_matrix, value_matrix, query_norm_gain, key_gain, block_mask
):
    position = lax.axis_index("seq")
    images = lax.broadcasted_iota(jnp.int32, (1, block_mask.shape[1], REACH), 1)
    wanted = position - lax.broadcasted_iota(jnp.int32, (1, block_mask.shape[1], REACH), 2)
    is_open = jnp.sum(jnp.where(images == wanted, block_mask[:, :, None], 0), axis=1)
    is_open = jnp.repeat(is_open.astype(jnp.float32), BLOCK, axis=0)
    query_gain = (query_norm_gain * SCORE_SCALE).reshape(1, HEAD_SIZE)
    key_gain = key_gain.reshape(1, HEAD_SIZE)

    def projected(row_parts, name):
        return project(row_parts, key_matrix, value_matrix, key_gain, "project_" + name)

    def reached(block, wraps=True):
        return [block] + [turned(block, "seq", by, wraps) for by in range(1, REACH)]

    left = turned(vision, "tp", 1)
    right = turned(vision, "tp", -1)
    own = projected([vision], "own")
    own_blocks = reached(own, wraps=False)
    normed, *carried = attend(
        text_query_matrix, own_blocks, is_open, query_gain, None, False, "attend_own"
    )

    half = vision.shape[1] * 13 // 32
    right = after(right, carried)
    last_half = turned(right[:, half:], "tp", -1)
    left = after(left, carried)
    first_half = turned(left[:, :half], "tp", 1)
    sides = projected([left, right], "sides")
    side_blocks = reached(sides)
    last_half = after(last_half, sides)
    across = project_by_halves(
        first_half, last_half, key_matrix, value_matrix, key_gain, "project_across"
    )
    across_blocks = reached(across)
    side_blocks = after(side_blocks, across)
    carried = attend(normed, side_blocks, is_open, None, carried, False, "attend_sides")
    across_blocks = after(across_blocks, carried)
    (result,) = attend(normed, across_blocks, is_open, None, carried, True, "attend_across")
    return result


def solution(mesh):
    placed = (
        P("seq", "tp"),
        P(("seq", "tp"), None),
        P(None, "tp"),
        P(None, "tp"),
        P(),
        P(),
        P("seq", None),
    )
    return jax.shard_map(
        body, mesh=mesh, in_specs=placed, out_specs=P("seq", "tp"), check_vma=False
    )
```

```python
import functools
import math

import jax
import jax.numpy as jnp
from jax import lax
from jax.experimental import pallas as pl
from jax.experimental.pallas import tpu as pltpu
from jax.sharding import PartitionSpec as P

HEAD_SIZE = 128
REACH = 4
BLOCK = 64
EPS = 1e-05
SCORE_SCALE = HEAD_SIZE ** (-0.5) * math.log2(math.e)
PROJECT_VMEM = 8 * 1024 * 1024
ATTEND_VMEM = 20 * 1024 * 1024
WHOLE = pl.BlockSpec(memory_space=pltpu.VMEM)
IN_PLACE = pl.BlockSpec(memory_space=pl.ANY)
HEADS_OUT = 4


def turned(value, axis, by, wraps=True):
    length = lax.axis_size(axis)
    pairs = [(i, (i + by) % length) for i in range(length) if wraps or i + by < length]
    return lax.ppermute(value, axis, pairs)


def write_keys_values(keys, values, gain_ref, out_ref):
    width = keys.shape[1]
    for head in range(width // HEAD_SIZE):
        at = slice(head * HEAD_SIZE, (head + 1) * HEAD_SIZE)
        own = keys[:, at]
        mean = jnp.mean(own * own, axis=-1, keepdims=True)
        out_ref[:, at] = (own * lax.rsqrt(mean + EPS) * gain_ref[...]).astype(out_ref.dtype)
    out_ref[:, width:] = values.astype(out_ref.dtype)


def project_cost(rows, key_matrix):
    size = math.prod(key_matrix.shape)
    return pl.CostEstimate(flops=4 * rows * size, transcendentals=0, bytes_accessed=4 * size)


def project_kernel(*refs):
    *row_refs, key_ref, value_ref, gain_ref, out_ref = refs
    rows = [ref[...] for ref in row_refs]
    rows = rows[0] if len(rows) == 1 else jnp.concatenate(rows, axis=0)
    keys = jnp.dot(rows, key_ref[...], preferred_element_type=jnp.float32)
    values = jnp.dot(rows, value_ref[...], preferred_element_type=jnp.float32)
    write_keys_values(keys, values, gain_ref, out_ref)


def project(row_parts, key_matrix, value_matrix, key_gain, name):
    width = key_matrix.shape[1]
    rows = sum(each.shape[0] for each in row_parts)
    return pl.pallas_call(
        project_kernel,
        out_shape=jax.ShapeDtypeStruct((rows, 2 * width), jnp.bfloat16),
        in_specs=[WHOLE] * (len(row_parts) + 3),
        out_specs=WHOLE,
        cost_estimate=project_cost(rows, key_matrix),
        compiler_params=pltpu.CompilerParams(vmem_limit_bytes=PROJECT_VMEM),
        name=name,
    )(*row_parts, key_matrix, value_matrix, key_gain)


def last_half_kernel(rows_ref, key_ref, value_ref, out_ref):
    before, width = key_ref.shape[0] - rows_ref.shape[1], key_ref.shape[1]
    rows = rows_ref[...]
    out_ref[:, :width] = jnp.dot(rows, key_ref[before:], preferred_element_type=jnp.float32)
    out_ref[:, width:] = jnp.dot(rows, value_ref[before:], preferred_element_type=jnp.float32)


def first_half_kernel(rows_ref, sums_ref, key_ref, value_ref, gain_ref, out_ref):
    depth, width = rows_ref.shape[1], key_ref.shape[1]
    rows = rows_ref[...]
    keys = jnp.dot(rows, key_ref[:depth], preferred_element_type=jnp.float32)
    values = jnp.dot(rows, value_ref[:depth], preferred_element_type=jnp.float32)
    write_keys_values(
        sums_ref[:, :width] + keys, sums_ref[:, width:] + values, gain_ref, out_ref
    )


def project_by_halves(first_half, last_half, key_matrix, value_matrix, key_gain, name):
    rows, width = first_half.shape[0], key_matrix.shape[1]
    params = dict(
        out_specs=WHOLE,
        cost_estimate=project_cost(rows // 2, key_matrix),
        compiler_params=pltpu.CompilerParams(vmem_limit_bytes=PROJECT_VMEM),
    )
    sums = pl.pallas_call(
        last_half_kernel,
        out_shape=jax.ShapeDtypeStruct((rows, 2 * width), jnp.float32),
        in_specs=[WHOLE] * 3,
        name=name + "_last_half",
        **params,
    )(last_half, key_matrix, value_matrix)
    first_half = after(first_half, sums)
    return pl.pallas_call(
        first_half_kernel,
        out_shape=jax.ShapeDtypeStruct((rows, 2 * width), jnp.bfloat16),
        in_specs=[WHOLE] * 5,
        name=name + "_first_half",
        **params,
    )(first_half, sums, key_matrix, value_matrix, key_gain)


def attend_kernel(first, last, kv_heads, *refs):
    refs = list(refs)
    copies = []
    if last:
        sems, held = refs.pop(), refs.pop()
    query_ref = refs.pop(0)
    block_refs = [refs.pop(0) for _ in range(REACH)]
    open_ref = refs.pop(0)
    if first:
        gain_ref, normed_ref = refs.pop(0), refs.pop(0)
    else:
        sums_in, totals_in = refs.pop(0), refs.pop(0)
    rows = query_ref.shape[0]
    count = block_refs[0].shape[0]
    group = query_ref.shape[1] // HEAD_SIZE // kv_heads
    image = lax.broadcasted_iota(jnp.int32, (rows, REACH * count), 1) // count
    is_open = jnp.zeros((rows, REACH * count), jnp.float32)
    for at in range(REACH):
        is_open = jnp.where(image == at, open_ref[:, at : at + 1], is_open)
    is_open = jnp.concatenate([is_open] * group, axis=0)
    lane = lax.broadcasted_iota(jnp.int32, (rows, HEAD_SIZE), 1)
    totals = jnp.zeros((rows, HEAD_SIZE), jnp.float32)

    def columns(head):
        return slice(head * HEAD_SIZE, (head + 1) * HEAD_SIZE)

    for kv_head in range(kv_heads):
        heads = range(kv_head * group, (kv_head + 1) * group)
        keys = jnp.concatenate([ref[:, columns(kv_head)] for ref in block_refs], axis=0)
        values = jnp.concatenate(
            [ref[:, columns(kv_heads + kv_head)] for ref in block_refs], axis=0
        )
        values = jnp.concatenate([values, jnp.ones_like(values)], axis=1)
        queries = []
        for head in heads:
            query = query_ref[:, columns(head)]
            if first:
                raw = query.astype(jnp.float32)
                mean = jnp.mean(raw * raw, axis=-1, keepdims=True)
                query = (raw * lax.rsqrt(mean + EPS) * gain_ref[...]).astype(jnp.bfloat16)
                normed_ref[:, columns(head)] = query
            queries.append(query)
        scores = lax.dot_general(
            jnp.concatenate(queries, axis=0),
            keys,
            (((1,), (1,)), ((), ())),
            preferred_element_type=jnp.float32,
        )
        weights = (jnp.exp2(scores) * is_open).astype(jnp.bfloat16)
        both = jnp.dot(weights, values, preferred_element_type=jnp.float32)
        for at, head in enumerate(heads):
            sums = both[at * rows : (at + 1) * rows, :HEAD_SIZE]
            total = both[at * rows : (at + 1) * rows, HEAD_SIZE:]
            if not first:
                sums = sums + sums_in[:, columns(head)]
                total = total + totals_in[:, head : head + 1]
            if last:
                safe = jnp.where(total > 0, total, jnp.ones_like(total))
                inverse = pl.reciprocal(safe, approx=True)
                inverse = inverse * (2.0 - safe * inverse)
                held[:, columns(head)] = (sums * inverse).astype(jnp.bfloat16)
                if head % HEADS_OUT == HEADS_OUT - 1:
                    part = pl.ds((head + 1 - HEADS_OUT) * HEAD_SIZE, HEADS_OUT * HEAD_SIZE)
                    copies.append(
                        pltpu.make_async_copy(
                            held.at[:, part], refs[0].at[:, part], sems.at[head // HEADS_OUT]
                        )
                    )
                    copies[-1].start()
            else:
                refs[0][:, columns(head)] = sums
                totals = jnp.where(lane == head, total, totals)
    if not last:
        refs[1][...] = totals
    for copy in copies:
        copy.wait()


def attend_cost(rows, width, keys):
    return pl.CostEstimate(
        flops=10 * rows * width * keys,
        transcendentals=rows * width // HEAD_SIZE * keys,
        bytes_accessed=2 * rows * width,
    )


def attend(query, blocks, is_open, gain, carried, last, name):
    first = carried is None
    rows, width = query.shape
    kv_heads = blocks[0].shape[1] // (2 * HEAD_SIZE)
    operands = [query, *blocks, is_open] + ([gain] if first else list(carried))
    scratch_shapes = []
    if last:
        out_shape = [jax.ShapeDtypeStruct((rows, width), jnp.bfloat16)]
        scratch_shapes.append(pltpu.VMEM((rows, width), jnp.bfloat16))
        scratch_shapes.append(pltpu.SemaphoreType.DMA((width // (HEADS_OUT * HEAD_SIZE),)))
    else:
        out_shape = [
            jax.ShapeDtypeStruct((rows, width), jnp.float32),
            jax.ShapeDtypeStruct((rows, HEAD_SIZE), jnp.float32),
        ]
    if first:
        out_shape.insert(0, jax.ShapeDtypeStruct((rows, width), jnp.bfloat16))
    return pl.pallas_call(
        functools.partial(attend_kernel, first, last, kv_heads),
        out_shape=out_shape,
        in_specs=[WHOLE] * len(operands),
        out_specs=[IN_PLACE if last else WHOLE] * len(out_shape),
        scratch_shapes=scratch_shapes,
        cost_estimate=attend_cost(rows, width, REACH * blocks[0].shape[0]),
        compiler_params=pltpu.CompilerParams(vmem_limit_bytes=ATTEND_VMEM),
        name=name,
    )(*operands)


def after(values, *others):
    return lax.optimization_barrier((values, others))[0]


def body(
    text_query_matrix, vision, key_matrix, value_matrix, query_norm_gain, key_gain, block_mask
):
    position = lax.axis_index("seq")
    images = lax.broadcasted_iota(jnp.int32, (1, block_mask.shape[1], REACH), 1)
    wanted = position - lax.broadcasted_iota(jnp.int32, (1, block_mask.shape[1], REACH), 2)
    is_open = jnp.sum(jnp.where(images == wanted, block_mask[:, :, None], 0), axis=1)
    is_open = jnp.repeat(is_open.astype(jnp.float32), BLOCK, axis=0)
    query_gain = (query_norm_gain * SCORE_SCALE).reshape(1, HEAD_SIZE)
    key_gain = key_gain.reshape(1, HEAD_SIZE)

    def projected(row_parts, name):
        return project(row_parts, key_matrix, value_matrix, key_gain, "project_" + name)

    def reached(block, wraps=True):
        return [block] + [turned(block, "seq", by, wraps) for by in range(1, REACH)]

    left = turned(vision, "tp", 1)
    right = turned(vision, "tp", -1)
    own = projected([vision], "own")
    own_blocks = reached(own, wraps=False)
    normed, *carried = attend(
        text_query_matrix, own_blocks, is_open, query_gain, None, False, "attend_own"
    )

    half = vision.shape[1] * 13 // 32
    right = after(right, carried)
    last_half = turned(right[:, half:], "tp", -1)
    left = after(left, carried)
    first_half = turned(left[:, :half], "tp", 1)
    sides = projected([left, right], "sides")
    side_blocks = reached(sides)
    last_half = after(last_half, sides)
    across = project_by_halves(
        first_half, last_half, key_matrix, value_matrix, key_gain, "project_across"
    )
    across_blocks = reached(across)
    side_blocks = after(side_blocks, across)
    carried = attend(normed, side_blocks, is_open, None, carried, False, "attend_sides")
    across_blocks = after(across_blocks, carried)
    (result,) = attend(normed, across_blocks, is_open, None, carried, True, "attend_across")
    return result


def solution(mesh):
    placed = (
        P("seq", "tp"),
        P(("seq", "tp"), None),
        P(None, "tp"),
        P(None, "tp"),
        P(),
        P(),
        P("seq", None),
    )
    return jax.shard_map(
        body, mesh=mesh, in_specs=placed, out_specs=P("seq", "tp"), check_vma=False
    )
```
